32 devices in a mesh: trainer: 8 (over y, x, core), depth: 4 (over z).
Axes of the slice: x: 2, y: 2, z: 4, core: 2. Of those that a mesh axis runs over, the one named last changes fastest.
Arguments:
- latent: bfloat16 [8, 8, 16, 16, 256], P('trainer', 'depth'), may hold values from -6 to 6
- gen_first: float32 [8, 256, 8192], P('trainer', 'depth'), may hold values from -0.125 to 0.125
- gen_second: float32 [8, 128, 4096], P('trainer', 'depth'), may hold values from -0.1875 to 0.1875
- critic: bfloat16 [8, 4096, 128], P('trainer'), may hold values from -0.09375 to 0.09375
- partner: int32 [8], replicated, may hold values from 0 to 7, as said below
Outputs:
- judged: bfloat16 [8, 2, 16, 32, 32, 128], P('trainer', None, 'depth')
The draws below stay inside these ranges and needn't reach their ends.
Inputs may be any that keep to these rules, and one draw needn't show every extreme that they name: partner[t] = t XOR m for every t, with one m for the whole array, 1 <= m < 8; so partner[partner[t]] = t and no trainer is its own partner.
All inputs are finite; a program needn't handle non-finite values.
Results may differ from the reference program's by a relative error of at most 0.0071.
Values may be sent and summed in bfloat16 or wider, within the bound.
A program may use at most 128 MiB of HBM per device.

```python
import jax
import jax.numpy as jnp
from jax import lax

C0 = 256
C1 = 128
C2 = 64
C3 = 128
LAT_HW = 16
TRAINERS = 8
LAT_D = 8


def draw_partner(key, part):
    offset = jax.random.randint(key, (), 1, TRAINERS).astype(jnp.int32)
    return jnp.bitwise_xor(jnp.arange(TRAINERS, dtype=jnp.int32), offset)


def block_scale(own_key, shape, cuts, least, high):
    def one(axis_at, blocks):
        draws = jax.random.uniform(jax.random.fold_in(jax.random.fold_in(own_key, 6), axis_at), (blocks,), jnp.float32, least / len(cuts), high / len(cuts))
        return jnp.repeat(jnp.exp(draws), shape[axis_at] // blocks).reshape((-1,) + (1,) * (len(shape) - axis_at - 1))

    gain = one(*cuts[0])
    for cut in cuts[1:]:
        gain = gain * one(*cut)
    return gain


def bell_draw(key, extent, scale, reach, shards=(), kind=jnp.bfloat16):
    factor_of = block_scale(key, extent, shards, -0.22, 0.18) if shards else 1.0
    values = jax.random.normal(key, extent, jnp.float32) * scale * factor_of
    return jnp.minimum(jnp.maximum(values, -reach), reach).astype(kind)


def setup_inputs(seed: int = 0) -> dict:
    arg_keys = jax.random.split(jax.random.key(seed), 6)
    return {
        "latent": bell_draw(arg_keys[0], (TRAINERS, LAT_D, LAT_HW, LAT_HW, C0), 1.0, 6.0, ((0, 8), (1, 4))),
        "gen_first": bell_draw(arg_keys[1], (TRAINERS, C0, 64 * C1), (8 * C0) ** -0.5, 0.125, ((0, 8), (1, 4)), jnp.float32),
        "gen_second": bell_draw(arg_keys[2], (TRAINERS, C1, 64 * C2), (8 * C1) ** -0.5, 0.1875, ((0, 8), (1, 4)), jnp.float32),
        "critic": bell_draw(arg_keys[3], (TRAINERS, 64 * C2, C3), (64 * C2) ** -0.5, 0.09375, ((0, 8),)),
        "partner": draw_partner(jax.random.fold_in(arg_keys[5], 71), 0),
    }


leak_slope = 0.2


def product(left, right):
    return jnp.dot(left.astype(jnp.float32), right.astype(jnp.float32), precision=lax.Precision.HIGHEST, preferred_element_type=jnp.float32)


def alternate(blocks):
    stacked = jnp.stack([jnp.stack([jnp.stack(pair_w, 0) for pair_w in pair_h], 0) for pair_h in blocks], 0)
    planes, height, across, channels = blocks[0][0][0].shape
    reordered = jnp.transpose(stacked, (3, 0, 4, 1, 5, 2, 6))
    return reordered.reshape(2 * planes, 2 * height, 2 * across, channels)


def transposed(volume, kernel):
    planes = volume.shape[0] - 2
    height = volume.shape[1]
    across = volume.shape[2]
    in_channels = volume.shape[3]
    padded = jnp.pad(volume, ((0, 0), (1, 1), (1, 1), (0, 0)))
    flipped = jnp.flip(kernel, (0, 1, 2))
    blocks = []
    for along_depth in (0, 1):
        height_blocks = []
        for along_height in (0, 1):
            width_blocks = []
            for along_width in (0, 1):
                columns = []
                weights = []
                for depth_tap in (0, 1):
                    for height_tap in (0, 1):
                        for width_tap in (0, 1):
                            depth_start = along_depth + depth_tap
                            height_start = along_height + height_tap
                            width_start = along_width + width_tap
                            columns.append(padded[depth_start:depth_start + planes, height_start:height_start + height, width_start:width_start + across])
                            weights.append(flipped[along_depth + 2 * depth_tap, along_height + 2 * height_tap, along_width + 2 * width_tap])
                gathered = jnp.concatenate(columns, axis=3).reshape(-1, 8 * in_channels)
                stacked = jnp.concatenate(weights, axis=0)
                result = product(gathered, stacked)
                width_blocks.append(result.reshape(planes, height, across, -1))
            height_blocks.append(width_blocks)
        blocks.append(height_blocks)
    return alternate(blocks)


def strided(volume, kernel):
    out_planes = (volume.shape[0] - 2) // 2
    out_height = volume.shape[1] // 2
    out_across = volume.shape[2] // 2
    in_channels = volume.shape[3]
    padded = jnp.pad(volume, ((0, 0), (1, 1), (1, 1), (0, 0)))
    total = jnp.zeros((out_planes * out_height * out_across, kernel.shape[4]), jnp.float32)
    for depth_tap in range(4):
        for height_tap in range(4):
            columns = [padded[depth_tap:depth_tap + 2 * out_planes:2, height_tap:height_tap + 2 * out_height:2, width_tap:width_tap + 2 * out_across:2] for width_tap in range(4)]
            gathered = jnp.concatenate(columns, axis=3).reshape(-1, 4 * in_channels)
            total = total + product(gathered, kernel[depth_tap, height_tap].reshape(4 * in_channels, -1))
    return total.reshape(out_planes, out_height, out_across, -1)


def unfold(weight):
    in_channels = weight.shape[0]
    shaped = weight.reshape(in_channels, 4, 4, 4, weight.shape[1] // 64)
    return jnp.transpose(shaped, (1, 2, 3, 0, 4))


def pad_depth(volume):
    return jnp.pad(volume, ((1, 1), (0, 0), (0, 0), (0, 0)))


def generate(seed_planes, first_weight, second_weight):
    first_kernel = unfold(first_weight.astype(jnp.bfloat16))
    second_kernel = unfold(second_weight.astype(jnp.bfloat16))
    hidden = jnp.maximum(transposed(pad_depth(seed_planes), first_kernel), 0.0).astype(jnp.bfloat16)
    density = jnp.tanh(transposed(pad_depth(hidden), second_kernel)).astype(jnp.bfloat16)
    return density


def judge(density, critic_kernel):
    scored = strided(pad_depth(density), critic_kernel)
    return jnp.where(scored > 0, scored, leak_slope * scored).astype(jnp.bfloat16)


def reference(latent, gen_first, gen_second, critic, partner):
    def one_trainer(trainer_index):
        mate_index = partner[trainer_index]
        seed_planes = latent[trainer_index]
        critic_kernel = critic[trainer_index].reshape(4, 4, 4, C2, C3)
        own_density = generate(seed_planes, gen_first[trainer_index], gen_second[trainer_index])
        mate_density = generate(seed_planes, gen_first[mate_index], gen_second[mate_index])
        return jnp.stack([judge(own_density, critic_kernel), judge(mate_density, critic_kernel)])

    return lax.map(one_trainer, jnp.arange(TRAINERS, dtype=jnp.int32))
```

```python
import functools

import jax
import jax.numpy as jnp
from jax import lax
from jax.experimental import pallas as pl
from jax.experimental.pallas import tpu as pltpu
from jax.sharding import PartitionSpec as P

leak_slope = 0.2
phases = [(pd, ph) for pd in (0, 1) for ph in (0, 1)]
taps = [(td, th) for td in (0, 1) for th in (0, 1)]
budget = 56 * 2**20


def exchanged(value, offset, order):
    count = lax.axis_size("trainer")
    for bit in order:
        pairs = [(source, source ^ (1 << bit)) for source in range(count)]
        moved = lax.ppermute(value, "trainer", pairs)
        chosen = jnp.bitwise_and(jnp.right_shift(offset, bit), 1) == 1
        value = jnp.where(chosen, moved, value)
    return value


def with_halo(block, dim):
    count = lax.axis_size("depth")
    forward = [(i, i + 1) for i in range(count - 1)]
    backward = [(i + 1, i) for i in range(count - 1)]
    size = block.shape[dim]
    low = lax.ppermute(lax.slice_in_dim(block, size - 1, size, axis=dim), "depth", forward)
    high = lax.ppermute(lax.slice_in_dim(block, 0, 1, axis=dim), "depth", backward)
    return jnp.concatenate([low, block, high], axis=dim)


def zeros_like_part(part):
    return jnp.zeros(part.shape, part.dtype)


def first_layer(pd, flags_ref, lat_ref, w_ref, out_ref, wide_ref, *, ph):
    jobs, planes, rows, cells, lanes = out_ref.shape
    c0 = w_ref.shape[0]
    c1 = lanes // 4
    for t in range(4):
        k = [w_ref[:, (4 * t + j) * c1 : (4 * t + j + 1) * c1] for j in range(4)]
        none = zeros_like_part(k[0])
        base = 3 * c0 * t
        wide_ref[base : base + c0, :] = jnp.concatenate([k[3], none], axis=1)
        wide_ref[base + c0 : base + 2 * c0, :] = jnp.concatenate([k[1], k[2]], axis=1)
        wide_ref[base + 2 * c0 : base + 3 * c0, :] = jnp.concatenate([none, k[0]], axis=1)
    edge = 0 if pd == 1 else planes - 1
    inside = flags_ref[0] if pd == 1 else flags_ref[1]

    def plane(n, carry):
        parts = [
            lat_ref[:, n + td, th + ph : th + ph + rows].reshape(jobs * rows * cells, 3 * c0)
            for td, th in taps
        ]
        total = jnp.dot(
            jnp.concatenate(parts, axis=1), wide_ref[...], preferred_element_type=jnp.float32
        )
        keep = jnp.logical_or(n != edge, inside == 1)
        total = jnp.where(keep, jnp.maximum(total, 0.0), 0.0)
        total = total.reshape(jobs * rows, cells, 2 * c1)
        even, odd = total[:, :, :c1], total[:, :, c1:]
        place = lax.broadcasted_iota(jnp.int32, even.shape, 1)
        before = jnp.where(place == 0, 0.0, pltpu.roll(odd, 1, 1))
        after = jnp.where(place == cells - 1, 0.0, pltpu.roll(even, cells - 1, 1))
        packed = jnp.concatenate([before, even, odd, after], axis=2).astype(jnp.bfloat16)
        out_ref[:, n] = packed.reshape(jobs, rows, cells, lanes)
        return carry

    lax.fori_loop(0, planes, plane, 0)


def hidden_part(pd, ph, flags, windows, weight):
    jobs, planes, rows, cells, lanes = windows.shape
    c1 = weight.shape[1] // 16
    out_shape = (jobs, planes - 1, rows - 2, cells, 4 * c1)
    flops = 2 * jobs * (planes - 1) * (rows - 2) * cells * 4 * lanes * 2 * c1
    return pl.pallas_call(
        functools.partial(first_layer, pd, ph=ph),
        out_shape=jax.ShapeDtypeStruct(out_shape, jnp.bfloat16),
        in_specs=[
            pl.BlockSpec(memory_space=pltpu.SMEM),
            pl.BlockSpec(memory_space=pltpu.VMEM),
            pl.BlockSpec(memory_space=pltpu.VMEM),
        ],
        out_specs=pl.BlockSpec(memory_space=pltpu.VMEM),
        scratch_shapes=[pltpu.VMEM((4 * lanes, 2 * c1), jnp.bfloat16)],
        compiler_params=pltpu.CompilerParams(vmem_limit_bytes=budget),
        cost_estimate=pl.CostEstimate(
            flops=flops, bytes_accessed=2 * (windows.size + weight.size), transcendentals=0
        ),
        name=f"hidden_{pd}{ph}",
    )(flags, windows, weight)


def rest(low_end, high_end, flags_ref, p00, p01, p10, p11, w_ref, critic_ref, out_ref,
         hid, wide2, img, wide3, stage):
    part_refs = {(0, 0): p00, (0, 1): p01, (1, 0): p10, (1, 1): p11}
    planes2, rows2, cells, lanes = hid.shape
    rows2 = rows2 - 2
    c1 = lanes // 4
    c2 = c1 // 2
    out_planes = out_ref.shape[0]
    c3 = out_ref.shape[3]

    empty = jnp.zeros((cells, lanes), jnp.bfloat16)
    for q in range(planes2):
        absolute = q + low_end[1]
        pd = 1 - absolute % 2
        n = absolute // 2
        pair = jnp.stack([part_refs[(pd, 0)][0, n], part_refs[(pd, 1)][0, n]], axis=1)
        hid[q, 1 : rows2 + 1] = pair.reshape(rows2, cells, lanes)
        hid[q, 0] = empty
        hid[q, rows2 + 1] = empty

    lane = lax.broadcasted_iota(jnp.int32, (c1, 4 * c2), 1)
    for index, (pd, ph) in enumerate(phases):
        for t, (td, th) in enumerate(taps):
            tap = (3 - pd - 2 * td) * 4 + 3 - ph - 2 * th
            k = w_ref[:, tap * 4 * c2 : (tap + 1) * 4 * c2].astype(jnp.float32)
            down = pltpu.roll(k, 3 * c2, 1)
            up = pltpu.roll(k, c2, 1)
            blocks = [
                jnp.where(lane < c2, up, 0.0),
                jnp.where(lane < 3 * c2, down, 0.0),
                jnp.where(lane >= c2, up, 0.0),
                jnp.where(lane >= 3 * c2, down, 0.0),
            ]
            base = t * 4 * c1
            for j in range(4):
                wide2[index, base + j * c1 : base + (j + 1) * c1, :] = blocks[j].astype(jnp.bfloat16)

    none = jnp.zeros((c2, c3), jnp.bfloat16)
    for t in range(16):
        base = t * 6 * c2
        k = [critic_ref[(4 * t + j) * c2 : (4 * t + j + 1) * c2, :] for j in range(4)]
        left = [k[1], k[2], k[3], none, none, k[0]]
        right = [none, k[0], k[1], k[2], k[3], none]
        for j in range(6):
            wide3[base + j * c2 : base + (j + 1) * c2, :c3] = left[j]
            wide3[base + j * c2 : base + (j + 1) * c2, c3:] = right[j]

    blank = jnp.zeros((cells, 6 * c2), jnp.bfloat16)
    for d in range(img.shape[0]):
        img[d, 0, 0] = blank
        img[d, rows2, 1] = blank

    for index, (pd, ph) in enumerate(phases):
        edge = 0 if pd == 1 else planes2 - 2
        ends = low_end[0] if pd == 1 else high_end
        inside = flags_ref[0] if pd == 1 else flags_ref[1]

        def plane(n, carry, index=index, pd=pd, ph=ph, edge=edge, ends=ends, inside=inside):
            parts = [
                hid[n + td, th + ph : th + ph + rows2].reshape(rows2 * cells, lanes)
                for td, th in taps
            ]
            total = jnp.dot(
                jnp.concatenate(parts, axis=1), wide2[index], preferred_element_type=jnp.float32
            )
            total = jnp.tanh(total)
            if ends:
                total = jnp.where(jnp.logical_or(n != edge, inside == 1), total, 0.0)
            total = total.reshape(rows2, cells, 4 * c2)
            first, second = total[:, :, : 2 * c2], total[:, :, 2 * c2 :]
            place = lax.broadcasted_iota(jnp.int32, first.shape, 1)
            column = lax.broadcasted_iota(jnp.int32, first.shape, 2)
            after = jnp.where(place == cells - 1, 0.0, pltpu.roll(first, cells - 1, 1))
            before = jnp.where(place == 0, 0.0, pltpu.roll(second, 1, 1))
            side = jnp.where(column < c2, after, before)
            packed = jnp.concatenate([first, second, side], axis=2).astype(jnp.bfloat16)
            if ph == 0:
                img[2 * n + 1 - pd, 0:rows2, 1] = packed
            else:
                img[2 * n + 1 - pd, 1 : rows2 + 1, 0] = packed
            return carry

        lax.fori_loop(0, planes2 - 1, plane, 0)

    def judged(m, carry):
        parts = [
            img[2 * m + kd, kh // 2 : kh // 2 + rows2, kh % 2].reshape(rows2 * cells, 6 * c2)
            for kd in range(4)
            for kh in range(4)
        ]
        total = jnp.dot(
            jnp.concatenate(parts, axis=1), wide3[...], preferred_element_type=jnp.float32
        )
        total = jnp.where(total > 0, total, leak_slope * total)
        count = rows2 * cells
        stage[pl.ds(0, count, stride=2), :] = total[:, :c3]
        stage[pl.ds(1, count, stride=2), :] = total[:, c3:]
        out_ref[m] = stage[...].reshape(rows2, 2 * cells, c3).astype(jnp.bfloat16)
        return carry

    lax.fori_loop(0, out_planes, judged, 0)


def judged_planes(job, start, count, flags, parts, second, critic, name):
    jobs, planes, rows, cells, lanes = parts[0].shape
    total_planes = 2 * (planes - 1)
    rows2 = 2 * rows
    c1 = second.shape[0]
    c2 = second.shape[1] // 64
    c3 = critic.shape[1]
    flops = 2 * rows2 * cells * 4 * c2 * ((count + 1) * 4 * 16 * c1 + count * 96 * c2)
    part_spec = pl.BlockSpec((1, planes, rows, cells, lanes), lambda i: (job, 0, 0, 0, 0))
    whole = lambda shape: pl.BlockSpec(shape, lambda i: (0,) * len(shape))
    out_shape = (count, rows2, 2 * cells, c3)
    return pl.pallas_call(
        functools.partial(rest, (start == 0, start), start + count == total_planes),
        grid=(1,),
        out_shape=jax.ShapeDtypeStruct(out_shape, jnp.bfloat16),
        in_specs=[
            pl.BlockSpec(memory_space=pltpu.SMEM),
            part_spec,
            part_spec,
            part_spec,
            part_spec,
            whole(second.shape),
            whole(critic.shape),
        ],
        out_specs=whole(out_shape),
        scratch_shapes=[
            pltpu.VMEM((count + 2, rows2 + 2, cells, lanes), jnp.bfloat16),
            pltpu.VMEM((4, 4 * lanes, 4 * c2), jnp.bfloat16),
            pltpu.VMEM((2 * count + 2, rows2 + 1, 2, cells, 6 * c2), jnp.bfloat16),
            pltpu.VMEM((96 * c2, 2 * c3), jnp.bfloat16),
            pltpu.VMEM((rows2 * cells * 2, c3), jnp.float32),
        ],
        compiler_params=pltpu.CompilerParams(vmem_limit_bytes=budget),
        cost_estimate=pl.CostEstimate(
            flops=flops, bytes_accessed=8 * parts[0].size, transcendentals=0
        ),
        name=name,
    )(flags, *parts, second, critic)


def windows_of(latents):
    padded = jnp.pad(latents, ((0, 0), (0, 0), (1, 1), (1, 1), (0, 0)))
    cells = latents.shape[3]
    return jnp.concatenate([padded[:, :, :, j : j + cells] for j in range(3)], axis=4)


def local(latent, gen_first, gen_second, critic, partner):
    trainer_index = lax.axis_index("trainer")
    offset = jnp.bitwise_xor(partner[trainer_index], trainer_index)
    rounds = lax.axis_size("trainer").bit_length() - 1
    orders = (
        tuple(range(1, rounds)) + (0,),
        tuple(range(rounds - 1, 0, -1)) + (0,),
    )
    z = lax.axis_index("depth")
    flags = jnp.stack([z > 0, z < lax.axis_size("depth") - 1]).astype(jnp.int32)

    c0, columns = gen_first.shape[1:]
    c1 = columns // 64
    shaped = gen_first[0].reshape(c0, 4, 4, 4 * c1)
    gathered = []
    for pd, ph in phases:
        blocks = [shaped[:, 3 - pd - 2 * td, 3 - ph - 2 * th] for td, th in taps]
        part = jnp.concatenate(blocks, axis=1).astype(jnp.bfloat16)
        gathered.append(lax.all_gather(part, "depth", axis=0, tiled=True))
    second = lax.all_gather(gen_second[0].astype(jnp.bfloat16), "depth", axis=0, tiled=True)

    mate_latent = exchanged(latent[0], offset, orders[0])
    windows = windows_of(with_halo(jnp.stack([latent[0], mate_latent]), 1))
    mate_critic = exchanged(critic[0], offset, orders[1])

    parts = [
        hidden_part(pd, ph, flags, windows, weight) for (pd, ph), weight in zip(phases, gathered)
    ]
    planes = 2 * latent.shape[1]
    half = planes // 2
    sent = judged_planes(1, 0, planes, flags, parts, second, mate_critic, "judged_mate")
    received = [
        exchanged(piece, offset, order)
        for piece, order in zip((sent[:half], sent[half:]), orders)
    ]
    own = [
        judged_planes(0, s, half, flags, parts, second, critic[0], "judged_own")
        for s in (0, half)
    ]
    return jnp.stack([jnp.concatenate(own), jnp.concatenate(received)])[None]


def solution(mesh):
    in_specs = (
        P("trainer", "depth", None, None, None),
        P("trainer", "depth", None),
        P("trainer", "depth", None),
        P("trainer", None, None),
        P(),
    )
    out_specs = P("trainer", None, "depth", None, None, None)
    return jax.shard_map(local, mesh=mesh, in_specs=in_specs, out_specs=out_specs, check_vma=False)
```

```python
import functools

import jax
import jax.numpy as jnp
from jax import lax
from jax.experimental import pallas as pl
from jax.experimental.pallas import tpu as pltpu
from jax.sharding import PartitionSpec as P

leak_slope = 0.2
phases = [(pd, ph) for pd in (0, 1) for ph in (0, 1)]
taps = [(td, th) for td in (0, 1) for th in (0, 1)]
budget = 56 * 2**20
mesh_ids = pl.DeviceIdType.MESH


def exchanged(value, offset, order):
    count = lax.axis_size("trainer")
    for bit in order:
        pairs = [(source, source ^ (1 << bit)) for source in range(count)]
        moved = lax.ppermute(value, "trainer", pairs)
        chosen = jnp.bitwise_and(jnp.right_shift(offset, bit), 1) == 1
        value = jnp.where(chosen, moved, value)
    return value


def hidden_kernel(
    bits, offset_ref, lat_ref, first_ref, second_ref, critic_ref,
    p00, p01, p10, p11, second_out, critic_out,
    first_buf, second_buf, lat_all, lat_cur, lat_got, critic_got, packed, wide, acc,
    first_send, first_recv, second_send, second_recv,
    lat_send, lat_recv, critic_send, critic_recv, halo_send, halo_recv,
):
    part_refs = (p00, p01, p10, p11)
    jobs, planes, rows, cells, lanes = p00.shape
    slab = planes - 1
    c1 = lanes // 4
    count = lax.axis_size("depth")
    z = lax.axis_index("depth")
    t = lax.axis_index("trainer")
    right, left = lax.rem(z + 1, count), lax.rem(z + count - 1, count)
    towards = (right, left)
    peers = [t + (1 << b) * (1 - 2 * lax.rem(t // (1 << b), 2)) for b in bits]
    cs = first_ref.shape[0]
    half = second_ref.shape[1] // 2
    quarter = first_ref.shape[1] // 4

    barrier = pltpu.get_barrier_semaphore()
    for there in towards:
        pl.semaphore_signal(barrier, inc=1, device_id={"depth": there}, device_id_type=mesh_ids)
    for peer in peers:
        pl.semaphore_signal(barrier, inc=1, device_id={"trainer": peer}, device_id_type=mesh_ids)

    for pd in (0, 1):
        for td in (0, 1):
            kd = 3 - pd - 2 * td
            piece = first_ref[:, kd * quarter : (kd + 1) * quarter]
            first_buf[pd, 0, td] = piece.astype(jnp.bfloat16)
        second_buf[pd, 0] = second_ref[:, pd * half : (pd + 1) * half].astype(jnp.bfloat16)
    lat_cur[...] = lat_ref[...]
    critic_out[...] = critic_ref[...]
    blank = jnp.zeros((cells, lat_ref.shape[3]), jnp.bfloat16)
    for j in range(jobs):
        for d in range(slab):
            lat_all[j, d + 1, 0] = blank
            lat_all[j, d + 1, rows + 1] = blank
    for d in range(slab):
        lat_all[0, d + 1, 1 : rows + 1] = lat_ref[d]
    pl.semaphore_wait(barrier, 2 + len(bits))

    def sent(src, dst, send, recv, **where):
        copy = pltpu.make_async_remote_copy(
            src_ref=src, dst_ref=dst, send_sem=send, recv_sem=recv,
            device_id=where, device_id_type=mesh_ids,
        )
        copy.start()
        return copy

    def halo(job):
        return [
            sent(lat_all.at[job, slab], lat_all.at[job, 0], halo_send.at[job, 0],
                 halo_recv.at[job, 0], depth=right),
            sent(lat_all.at[job, 1], lat_all.at[job, slab + 1], halo_send.at[job, 1],
                 halo_recv.at[job, 1], depth=left),
        ]

    def ring(step):
        copies = []
        for pd in (0, 1):
            for td in (0, 1):
                copies.append(
                    sent(first_buf.at[pd, step, td], first_buf.at[pd, step + 1, td],
                         first_send.at[pd, step, td], first_recv.at[pd, step, td],
                         depth=towards[pd])
                )
        for pd in (0, 1):
            copies.append(
                sent(second_buf.at[pd, step], second_buf.at[pd, step + 1],
                     second_send.at[pd, step], second_recv.at[pd, step], depth=towards[pd])
            )
        return copies

    def swap_latent(r):
        return sent(lat_cur, lat_got.at[r], lat_send.at[r], lat_recv.at[r], trainer=peers[r])

    def swap_critic(r):
        return sent(critic_out, critic_got.at[r], critic_send.at[r], critic_recv.at[r],
                    trainer=peers[r])

    def chosen(r):
        return offset_ref[bits[r]] == 1

    moving = swap_latent(0)
    halos = halo(0)
    moves = ring(0)
    for r in range(len(bits)):
        moving.wait()
        lat_cur[...] = jnp.where(chosen(r), lat_got[r], lat_cur[...])
        if r + 1 < len(bits):
            moving = swap_latent(r + 1)
    for d in range(slab):
        lat_all[1, d + 1, 1 : rows + 1] = lat_cur[d]
    halos += halo(1)
    critic_move = swap_critic(0)
    for copy in halos:
        copy.wait()
    for end, inside in ((0, z > 0), (slab + 1, z < count - 1)):
        lat_all[:, end] = jnp.where(inside, lat_all[:, end], jnp.zeros_like(lat_all[:, end]))

    per = 128 // cs
    group_rows = jobs * (rows + 1)

    def pack(n, carry):
        for s in range(count):
            tile, off = s * cs // 128 * 128, s * cs % 128
            for g in range(4 // per):
                center = None
                for i in range(per):
                    td, th = divmod(g * per + i, 2)
                    x = lat_all[:, n + td, th : th + rows + 1, :, tile : tile + 128]
                    x = x.astype(jnp.float32).reshape(group_rows * cells, 128)
                    shift = (i * cs - off) % 128
                    x = pltpu.roll(x, shift, 1) if shift else x
                    lane = lax.broadcasted_iota(jnp.int32, x.shape, 1)
                    center = x if center is None else jnp.where(lane < i * cs, center, x)
                center = center.reshape(group_rows, cells, 128)
                place = lax.broadcasted_iota(jnp.int32, center.shape, 1)
                before = jnp.where(place == 0, 0.0, pltpu.roll(center, 1, 1))
                after = jnp.where(place == cells - 1, 0.0, pltpu.roll(center, cells - 1, 1))
                for j, value in enumerate((before, center, after)):
                    base = j * 4 * cs + g * 128
                    packed[s, :, n, :, :, base : base + 128] = value.astype(jnp.bfloat16).reshape(
                        jobs, rows + 1, cells, 128
                    )
        return carry

    lax.fori_loop(0, planes, pack, 0)

    none = jnp.zeros((cs, c1), jnp.bfloat16)
    for step in range(count):
        if step:
            for copy in moves:
                copy.wait()
            if step < count - 1:
                moves = ring(step)
        for pd in (0, 1):
            owner = lax.rem(z + count - step, count) if pd == 0 else lax.rem(z + step, count)
            second_out[owner, :, pd * half : (pd + 1) * half] = second_buf[pd, step]
            for ph in (0, 1):
                for td, th in taps:
                    col = (3 - ph - 2 * th) * 4 * c1
                    k = [
                        first_buf[pd, step, td, :, col + j * c1 : col + (j + 1) * c1]
                        for j in range(4)
                    ]
                    for j, (a, b) in enumerate(((k[3], none), (k[1], k[2]), (none, k[0]))):
                        base = (4 * j + 2 * td + th) * cs
                        wide[base : base + cs, :c1] = a
                        wide[base : base + cs, c1:] = b

                def plane(n, carry, ph=ph, index=2 * pd + ph, owner=owner, step=step):
                    lhs = packed[owner, :, n, ph : ph + rows].reshape(
                        jobs * rows * cells, 12 * cs
                    )
                    total = jnp.dot(lhs, wide[...], preferred_element_type=jnp.float32)
                    acc[index, n] = total if step == 0 else acc[index, n] + total
                    return carry

                lax.fori_loop(0, planes, plane, 0)
        if step < len(bits):
            critic_move.wait()
            critic_out[...] = jnp.where(chosen(step), critic_got[step], critic_out[...])
            if step + 1 < len(bits):
                critic_move = swap_critic(step + 1)

    for index, (pd, ph) in enumerate(phases):
        edge = 0 if pd == 1 else planes - 1
        inside = z > 0 if pd == 1 else z < count - 1

        def finish(n, carry, index=index, edge=edge, inside=inside):
            keep = jnp.logical_or(n != edge, inside)
            total = jnp.where(keep, jnp.maximum(acc[index, n], 0.0), 0.0)
            total = total.reshape(jobs * rows, cells, 2 * c1)
            even, odd = total[:, :, :c1], total[:, :, c1:]
            place = lax.broadcasted_iota(jnp.int32, even.shape, 1)
            before = jnp.where(place == 0, 0.0, pltpu.roll(odd, 1, 1))
            after = jnp.where(place == cells - 1, 0.0, pltpu.roll(even, cells - 1, 1))
            result = jnp.concatenate([before, even, odd, after], axis=2).astype(jnp.bfloat16)
            part_refs[index][:, n] = result.reshape(jobs, rows, cells, lanes)
            return carry

        lax.fori_loop(0, planes, finish, 0)


def hidden_parts(offset_bits, latent, first, second, critic, bits):
    slab, rows, cells, c0 = latent.shape
    count = lax.axis_size("depth")
    cs, columns = first.shape
    c1 = columns // 64
    rounds = len(bits)
    part = jax.ShapeDtypeStruct((2, slab + 1, rows, cells, 4 * c1), jnp.bfloat16)
    in_vmem = pl.BlockSpec(memory_space=pltpu.VMEM)
    half = second.shape[1] // 2
    dma = pltpu.SemaphoreType.DMA
    flops = 2 * 2 * (slab + 1) * rows * cells * 4 * 12 * c0 * 2 * c1
    return pl.pallas_call(
        functools.partial(hidden_kernel, bits),
        out_shape=[part] * 4
        + [
            jax.ShapeDtypeStruct((count,) + second.shape, jnp.bfloat16),
            jax.ShapeDtypeStruct(critic.shape, jnp.bfloat16),
        ],
        in_specs=[pl.BlockSpec(memory_space=pltpu.SMEM)] + [in_vmem] * 4,
        out_specs=[in_vmem] * 6,
        scratch_shapes=[
            pltpu.VMEM((2, count, 2, cs, columns // 4), jnp.bfloat16),
            pltpu.VMEM((2, count, second.shape[0], half), jnp.bfloat16),
            pltpu.VMEM((2, slab + 2, rows + 2, cells, c0), jnp.bfloat16),
            pltpu.VMEM(latent.shape, jnp.bfloat16),
            pltpu.VMEM((rounds,) + latent.shape, jnp.bfloat16),
            pltpu.VMEM((rounds,) + critic.shape, jnp.bfloat16),
            pltpu.VMEM((count, 2, slab + 1, rows + 1, cells, 12 * cs), jnp.bfloat16),
            pltpu.VMEM((12 * cs, 2 * c1), jnp.bfloat16),
            pltpu.VMEM((4, slab + 1, 2 * rows * cells, 2 * c1), jnp.float32),
            dma((2, count - 1, 2)),
            dma((2, count - 1, 2)),
            dma((2, count - 1)),
            dma((2, count - 1)),
            dma((rounds,)),
            dma((rounds,)),
            dma((rounds,)),
            dma((rounds,)),
            dma((2, 2)),
            dma((2, 2)),
        ],
        compiler_params=pltpu.CompilerParams(
            vmem_limit_bytes=budget, collective_id=0, has_side_effects=True
        ),
        cost_estimate=pl.CostEstimate(flops=flops, bytes_accessed=2**24, transcendentals=0),
        name="hidden",
    )(offset_bits, latent, first, second, critic)


def rest(low_end, high_end, flags_ref, p00, p01, p10, p11, w_ref, critic_ref, out_ref,
         hid, wide2, img, wide3, stage):
    part_refs = {(0, 0): p00, (0, 1): p01, (1, 0): p10, (1, 1): p11}
    planes2, rows2, cells, lanes = hid.shape
    rows2 = rows2 - 2
    c1 = lanes // 4
    c2 = c1 // 2
    out_planes = out_ref.shape[0]
    c3 = out_ref.shape[3]

    empty = jnp.zeros((cells, lanes), jnp.bfloat16)
    for q in range(planes2):
        absolute = q + low_end[1]
        pd = 1 - absolute % 2
        n = absolute // 2
        pair = jnp.stack([part_refs[(pd, 0)][0, n], part_refs[(pd, 1)][0, n]], axis=1)
        hid[q, 1 : rows2 + 1] = pair.reshape(rows2, cells, lanes)
        hid[q, 0] = empty
        hid[q, rows2 + 1] = empty

    lane = lax.broadcasted_iota(jnp.int32, (c1, 4 * c2), 1)
    for index, (pd, ph) in enumerate(phases):
        for t, (td, th) in enumerate(taps):
            tap = (3 - pd - 2 * td) * 4 + 3 - ph - 2 * th
            k = w_ref[:, tap * 4 * c2 : (tap + 1) * 4 * c2].astype(jnp.float32)
            down = pltpu.roll(k, 3 * c2, 1)
            up = pltpu.roll(k, c2, 1)
            blocks = [
                jnp.where(lane < c2, up, 0.0),
                jnp.where(lane < 3 * c2, down, 0.0),
                jnp.where(lane >= c2, up, 0.0),
                jnp.where(lane >= 3 * c2, down, 0.0),
            ]
            base = t * 4 * c1
            for j in range(4):
                wide2[index, base + j * c1 : base + (j + 1) * c1, :] = blocks[j].astype(jnp.bfloat16)

    none = jnp.zeros((c2, c3), jnp.bfloat16)
    for t in range(16):
        base = t * 6 * c2
        k = [critic_ref[(4 * t + j) * c2 : (4 * t + j + 1) * c2, :] for j in range(4)]
        left = [k[1], k[2], k[3], none, none, k[0]]
        right = [none, k[0], k[1], k[2], k[3], none]
        for j in range(6):
            wide3[base + j * c2 : base + (j + 1) * c2, :c3] = left[j]
            wide3[base + j * c2 : base + (j + 1) * c2, c3:] = right[j]

    blank = jnp.zeros((cells, 6 * c2), jnp.bfloat16)
    for d in range(img.shape[0]):
        img[d, 0, 0] = blank
        img[d, rows2, 1] = blank

    for index, (pd, ph) in enumerate(phases):
        edge = 0 if pd == 1 else planes2 - 2
        ends = low_end[0] if pd == 1 else high_end
        inside = flags_ref[0] if pd == 1 else flags_ref[1]

        def plane(n, carry, index=index, pd=pd, ph=ph, edge=edge, ends=ends, inside=inside):
            parts = [
                hid[n + td, th + ph : th + ph + rows2].reshape(rows2 * cells, lanes)
                for td, th in taps
            ]
            total = jnp.dot(
                jnp.concatenate(parts, axis=1), wide2[index], preferred_element_type=jnp.float32
            )
            total = jnp.tanh(total)
            if ends:
                total = jnp.where(jnp.logical_or(n != edge, inside == 1), total, 0.0)
            total = total.reshape(rows2, cells, 4 * c2)
            first, second = total[:, :, : 2 * c2], total[:, :, 2 * c2 :]
            place = lax.broadcasted_iota(jnp.int32, first.shape, 1)
            column = lax.broadcasted_iota(jnp.int32, first.shape, 2)
            after = jnp.where(place == cells - 1, 0.0, pltpu.roll(first, cells - 1, 1))
            before = jnp.where(place == 0, 0.0, pltpu.roll(second, 1, 1))
            side = jnp.where(column < c2, after, before)
            packed = jnp.concatenate([first, second, side], axis=2).astype(jnp.bfloat16)
            if ph == 0:
                img[2 * n + 1 - pd, 0:rows2, 1] = packed
            else:
                img[2 * n + 1 - pd, 1 : rows2 + 1, 0] = packed
            return carry

        lax.fori_loop(0, planes2 - 1, plane, 0)

    def judged(m, carry):
        parts = [
            img[2 * m + kd, kh // 2 : kh // 2 + rows2, kh % 2].reshape(rows2 * cells, 6 * c2)
            for kd in range(4)
            for kh in range(4)
        ]
        total = jnp.dot(
            jnp.concatenate(parts, axis=1), wide3[...], preferred_element_type=jnp.float32
        )
        total = jnp.where(total > 0, total, leak_slope * total)
        count = rows2 * cells
        stage[pl.ds(0, count, stride=2), :] = total[:, :c3]
        stage[pl.ds(1, count, stride=2), :] = total[:, c3:]
        out_ref[m] = stage[...].reshape(rows2, 2 * cells, c3).astype(jnp.bfloat16)
        return carry

    lax.fori_loop(0, out_planes, judged, 0)


def judged_planes(job, start, count, flags, parts, second, critic, name):
    jobs, planes, rows, cells, lanes = parts[0].shape
    total_planes = 2 * (planes - 1)
    rows2 = 2 * rows
    c1 = second.shape[0]
    c2 = second.shape[1] // 64
    c3 = critic.shape[1]
    flops = 2 * rows2 * cells * 4 * c2 * ((count + 1) * 4 * 16 * c1 + count * 96 * c2)
    part_spec = pl.BlockSpec((1, planes, rows, cells, lanes), lambda i: (job, 0, 0, 0, 0))
    whole = lambda shape: pl.BlockSpec(shape, lambda i: (0,) * len(shape))
    out_shape = (count, rows2, 2 * cells, c3)
    return pl.pallas_call(
        functools.partial(rest, (start == 0, start), start + count == total_planes),
        grid=(1,),
        out_shape=jax.ShapeDtypeStruct(out_shape, jnp.bfloat16),
        in_specs=[
            pl.BlockSpec(memory_space=pltpu.SMEM),
            part_spec,
            part_spec,
            part_spec,
            part_spec,
            whole(second.shape),
            whole(critic.shape),
        ],
        out_specs=whole(out_shape),
        scratch_shapes=[
            pltpu.VMEM((count + 2, rows2 + 2, cells, lanes), jnp.bfloat16),
            pltpu.VMEM((4, 4 * lanes, 4 * c2), jnp.bfloat16),
            pltpu.VMEM((2 * count + 2, rows2 + 1, 2, cells, 6 * c2), jnp.bfloat16),
            pltpu.VMEM((96 * c2, 2 * c3), jnp.bfloat16),
            pltpu.VMEM((rows2 * cells * 2, c3), jnp.float32),
        ],
        compiler_params=pltpu.CompilerParams(vmem_limit_bytes=budget),
        cost_estimate=pl.CostEstimate(
            flops=flops, bytes_accessed=8 * parts[0].size, transcendentals=0
        ),
        name=name,
    )(flags, *parts, second, critic)


def local(latent, gen_first, gen_second, critic, partner):
    trainer_index = lax.axis_index("trainer")
    offset = jnp.bitwise_xor(partner[trainer_index], trainer_index)
    rounds = lax.axis_size("trainer").bit_length() - 1
    orders = (
        tuple(range(1, rounds)) + (0,),
        tuple(range(rounds - 1, 0, -1)) + (0,),
    )
    z = lax.axis_index("depth")
    flags = jnp.stack([z > 0, z < lax.axis_size("depth") - 1]).astype(jnp.int32)

    bits = orders[0]
    offset_bits = jnp.stack([jnp.bitwise_and(jnp.right_shift(offset, b), 1) for b in range(rounds)])
    *parts, second, mate_critic = hidden_parts(
        offset_bits, latent[0], gen_first[0], gen_second[0], critic[0], bits
    )
    second = second.reshape(-1, second.shape[2])
    planes = 2 * latent.shape[1]
    half = planes // 2
    sent = judged_planes(1, 0, planes, flags, parts, second, mate_critic, "judged_mate")
    received = [
        exchanged(piece, offset, order)
        for piece, order in zip((sent[:half], sent[half:]), orders)
    ]
    own = [
        judged_planes(0, s, half, flags, parts, second, critic[0], "judged_own")
        for s in (0, half)
    ]
    return jnp.stack([jnp.concatenate(own), jnp.concatenate(received)])[None]


def solution(mesh):
    in_specs = (
        P("trainer", "depth", None, None, None),
        P("trainer", "depth", None),
        P("trainer", "depth", None),
        P("trainer", None, None),
        P(),
    )
    out_specs = P("trainer", None, "depth", None, None, None)
    return jax.shard_map(local, mesh=mesh, in_specs=in_specs, out_specs=out_specs, check_vma=False)
```

```python
import functools

import jax
import jax.numpy as jnp
from jax import lax
from jax.experimental import pallas as pl
from jax.experimental.pallas import tpu as pltpu
from jax.sharding import PartitionSpec as P

leak_slope = 0.2
phases = [(pd, ph) for pd in (0, 1) for ph in (0, 1)]
taps = [(td, th) for td in (0, 1) for th in (0, 1)]
budget = 56 * 2**20
mesh_ids = pl.DeviceIdType.MESH


def hidden_kernel(
    bits, offset_ref, lat_ref, first_ref, second_ref, critic_ref,
    p00, p01, p10, p11, second_out, critic_out,
    first_buf, second_buf, lat_all, lat_cur, lat_got, critic_got, packed, wide, acc,
    first_send, first_recv, second_send, second_recv,
    lat_send, lat_recv, critic_send, critic_recv, halo_send, halo_recv,
):
    part_refs = (p00, p01, p10, p11)
    jobs, planes, rows, cells, lanes = p00.shape
    slab = planes - 1
    c1 = lanes // 4
    count = lax.axis_size("depth")
    z = lax.axis_index("depth")
    t = lax.axis_index("trainer")
    right, left = lax.rem(z + 1, count), lax.rem(z + count - 1, count)
    towards = (right, left)
    peers = [t + (1 << b) * (1 - 2 * lax.rem(t // (1 << b), 2)) for b in bits]
    cs = first_ref.shape[0]
    half = second_ref.shape[1] // 2
    quarter = first_ref.shape[1] // 4

    barrier = pltpu.get_barrier_semaphore()
    for there in towards:
        pl.semaphore_signal(barrier, inc=1, device_id={"depth": there}, device_id_type=mesh_ids)
    for peer in peers:
        pl.semaphore_signal(barrier, inc=1, device_id={"trainer": peer}, device_id_type=mesh_ids)

    for pd in (0, 1):
        for td in (0, 1):
            kd = 3 - pd - 2 * td
            piece = first_ref[:, kd * quarter : (kd + 1) * quarter]
            first_buf[pd, 0, td] = piece.astype(jnp.bfloat16)
        second_buf[pd, 0] = second_ref[:, pd * half : (pd + 1) * half].astype(jnp.bfloat16)
    lat_cur[...] = lat_ref[...]
    critic_out[...] = critic_ref[...]
    blank = jnp.zeros((cells, lat_ref.shape[3]), jnp.bfloat16)
    for j in range(jobs):
        for d in range(slab):
            lat_all[j, d + 1, 0] = blank
            lat_all[j, d + 1, rows + 1] = blank
    for d in range(slab):
        lat_all[0, d + 1, 1 : rows + 1] = lat_ref[d]
    pl.semaphore_wait(barrier, 2 + len(bits))

    def sent(src, dst, send, recv, **where):
        copy = pltpu.make_async_remote_copy(
            src_ref=src, dst_ref=dst, send_sem=send, recv_sem=recv,
            device_id=where, device_id_type=mesh_ids,
        )
        copy.start()
        return copy

    def halo(job):
        return [
            sent(lat_all.at[job, slab], lat_all.at[job, 0], halo_send.at[job, 0],
                 halo_recv.at[job, 0], depth=right),
            sent(lat_all.at[job, 1], lat_all.at[job, slab + 1], halo_send.at[job, 1],
                 halo_recv.at[job, 1], depth=left),
        ]

    def ring(step):
        copies = []
        for pd in (0, 1):
            for td in (0, 1):
                copies.append(
                    sent(first_buf.at[pd, step, td], first_buf.at[pd, step + 1, td],
                         first_send.at[pd, step, td], first_recv.at[pd, step, td],
                         depth=towards[pd])
                )
        for pd in (0, 1):
            copies.append(
                sent(second_buf.at[pd, step], second_buf.at[pd, step + 1],
                     second_send.at[pd, step], second_recv.at[pd, step], depth=towards[pd])
            )
        return copies

    def swap_latent(r):
        return sent(lat_cur, lat_got.at[r], lat_send.at[r], lat_recv.at[r], trainer=peers[r])

    def swap_critic(r):
        return sent(critic_out, critic_got.at[r], critic_send.at[r], critic_recv.at[r],
                    trainer=peers[r])

    def chosen(r):
        return offset_ref[bits[r]] == 1

    moving = swap_latent(0)
    halos = halo(0)
    moves = ring(0)
    for r in range(len(bits)):
        moving.wait()
        lat_cur[...] = jnp.where(chosen(r), lat_got[r], lat_cur[...])
        if r + 1 < len(bits):
            moving = swap_latent(r + 1)
    for d in range(slab):
        lat_all[1, d + 1, 1 : rows + 1] = lat_cur[d]
    halos += halo(1)
    critic_move = swap_critic(0)
    for copy in halos:
        copy.wait()
    for end, inside in ((0, z > 0), (slab + 1, z < count - 1)):
        lat_all[:, end] = jnp.where(inside, lat_all[:, end], jnp.zeros_like(lat_all[:, end]))

    per = 128 // cs
    group_rows = jobs * (rows + 1)

    def pack(n, carry):
        for s in range(count):
            tile, off = s * cs // 128 * 128, s * cs % 128
            for g in range(4 // per):
                center = None
                for i in range(per):
                    td, th = divmod(g * per + i, 2)
                    x = lat_all[:, n + td, th : th + rows + 1, :, tile : tile + 128]
                    x = x.astype(jnp.float32).reshape(group_rows * cells, 128)
                    shift = (i * cs - off) % 128
                    x = pltpu.roll(x, shift, 1) if shift else x
                    lane = lax.broadcasted_iota(jnp.int32, x.shape, 1)
                    center = x if center is None else jnp.where(lane < i * cs, center, x)
                center = center.reshape(group_rows, cells, 128)
                place = lax.broadcasted_iota(jnp.int32, center.shape, 1)
                before = jnp.where(place == 0, 0.0, pltpu.roll(center, 1, 1))
                after = jnp.where(place == cells - 1, 0.0, pltpu.roll(center, cells - 1, 1))
                for j, value in enumerate((before, center, after)):
                    base = j * 4 * cs + g * 128
                    packed[s, :, n, :, :, base : base + 128] = value.astype(jnp.bfloat16).reshape(
                        jobs, rows + 1, cells, 128
                    )
        return carry

    lax.fori_loop(0, planes, pack, 0)

    none = jnp.zeros((cs, c1), jnp.bfloat16)
    for step in range(count):
        if step:
            for copy in moves:
                copy.wait()
            if step < count - 1:
                moves = ring(step)
        for pd in (0, 1):
            owner = lax.rem(z + count - step, count) if pd == 0 else lax.rem(z + step, count)
            second_out[owner, :, pd * half : (pd + 1) * half] = second_buf[pd, step]
            for ph in (0, 1):
                for td, th in taps:
                    col = (3 - ph - 2 * th) * 4 * c1
                    k = [
                        first_buf[pd, step, td, :, col + j * c1 : col + (j + 1) * c1]
                        for j in range(4)
                    ]
                    for j, (a, b) in enumerate(((k[3], none), (k[1], k[2]), (none, k[0]))):
                        base = (4 * j + 2 * td + th) * cs
                        wide[base : base + cs, :c1] = a
                        wide[base : base + cs, c1:] = b

                def plane(n, carry, ph=ph, index=2 * pd + ph, owner=owner, step=step):
                    lhs = packed[owner, :, n, ph : ph + rows].reshape(
                        jobs * rows * cells, 12 * cs
                    )
                    total = jnp.dot(lhs, wide[...], preferred_element_type=jnp.float32)
                    acc[index, n] = total if step == 0 else acc[index, n] + total
                    return carry

                lax.fori_loop(0, planes, plane, 0)
        if step < len(bits):
            critic_move.wait()
            critic_out[...] = jnp.where(chosen(step), critic_got[step], critic_out[...])
            if step + 1 < len(bits):
                critic_move = swap_critic(step + 1)

    for index, (pd, ph) in enumerate(phases):
        edge = 0 if pd == 1 else planes - 1
        inside = z > 0 if pd == 1 else z < count - 1

        def finish(n, carry, index=index, edge=edge, inside=inside):
            keep = jnp.logical_or(n != edge, inside)
            total = jnp.where(keep, jnp.maximum(acc[index, n], 0.0), 0.0)
            total = total.reshape(jobs * rows, cells, 2 * c1)
            even, odd = total[:, :, :c1], total[:, :, c1:]
            place = lax.broadcasted_iota(jnp.int32, even.shape, 1)
            before = jnp.where(place == 0, 0.0, pltpu.roll(odd, 1, 1))
            after = jnp.where(place == cells - 1, 0.0, pltpu.roll(even, cells - 1, 1))
            result = jnp.concatenate([before, even, odd, after], axis=2).astype(jnp.bfloat16)
            part_refs[index][:, n] = result.reshape(jobs, rows, cells, lanes)
            return carry

        lax.fori_loop(0, planes, finish, 0)


def hidden_parts(offset_bits, latent, first, second, critic, bits):
    slab, rows, cells, c0 = latent.shape
    count = lax.axis_size("depth")
    cs, columns = first.shape
    c1 = columns // 64
    rounds = len(bits)
    part = jax.ShapeDtypeStruct((2, slab + 1, rows, cells, 4 * c1), jnp.bfloat16)
    in_vmem = pl.BlockSpec(memory_space=pltpu.VMEM)
    half = second.shape[1] // 2
    dma = pltpu.SemaphoreType.DMA
    flops = 2 * 2 * (slab + 1) * rows * cells * 4 * 12 * c0 * 2 * c1
    return pl.pallas_call(
        functools.partial(hidden_kernel, bits),
        out_shape=[part] * 4
        + [
            jax.ShapeDtypeStruct((count,) + second.shape, jnp.bfloat16),
            jax.ShapeDtypeStruct(critic.shape, jnp.bfloat16),
        ],
        in_specs=[pl.BlockSpec(memory_space=pltpu.SMEM)] + [in_vmem] * 4,
        out_specs=[in_vmem] * 6,
        scratch_shapes=[
            pltpu.VMEM((2, count, 2, cs, columns // 4), jnp.bfloat16),
            pltpu.VMEM((2, count, second.shape[0], half), jnp.bfloat16),
            pltpu.VMEM((2, slab + 2, rows + 2, cells, c0), jnp.bfloat16),
            pltpu.VMEM(latent.shape, jnp.bfloat16),
            pltpu.VMEM((rounds,) + latent.shape, jnp.bfloat16),
            pltpu.VMEM((rounds,) + critic.shape, jnp.bfloat16),
            pltpu.VMEM((count, 2, slab + 1, rows + 1, cells, 12 * cs), jnp.bfloat16),
            pltpu.VMEM((12 * cs, 2 * c1), jnp.bfloat16),
            pltpu.VMEM((4, slab + 1, 2 * rows * cells, 2 * c1), jnp.float32),
            dma((2, count - 1, 2)),
            dma((2, count - 1, 2)),
            dma((2, count - 1)),
            dma((2, count - 1)),
            dma((rounds,)),
            dma((rounds,)),
            dma((rounds,)),
            dma((rounds,)),
            dma((2, 2)),
            dma((2, 2)),
        ],
        compiler_params=pltpu.CompilerParams(
            vmem_limit_bytes=budget, collective_id=0, has_side_effects=True
        ),
        cost_estimate=pl.CostEstimate(flops=flops, bytes_accessed=2**24, transcendentals=0),
        name="hidden",
    )(offset_bits, latent, first, second, critic)


def judged_kernel(
    bits, offset_ref, p00, p01, p10, p11, w_ref, mate_critic_ref, critic_ref, out_ref,
    hid, wide2, img, wide3, stage, got, send_sem, recv_sem,
):
    part_refs = {(0, 0): p00, (0, 1): p01, (1, 0): p10, (1, 1): p11}
    planes2, rows2, cells, lanes = hid.shape
    rows2 = rows2 - 2
    c1 = lanes // 4
    c2 = c1 // 2
    out_planes, c3 = out_ref.shape[1], out_ref.shape[4]
    z = lax.axis_index("depth")
    t = lax.axis_index("trainer")
    rounds = len(bits[0])
    peers = [t + (1 << b) * (1 - 2 * lax.rem(t // (1 << b), 2)) for b in range(rounds)]
    barrier = pltpu.get_barrier_semaphore()
    for peer in peers:
        pl.semaphore_signal(barrier, inc=1, device_id={"trainer": peer}, device_id_type=mesh_ids)

    lane = lax.broadcasted_iota(jnp.int32, (c1, 4 * c2), 1)
    for index, (pd, ph) in enumerate(phases):
        for tap_index, (td, th) in enumerate(taps):
            tap = (3 - pd - 2 * td) * 4 + 3 - ph - 2 * th
            k = w_ref[:, tap * 4 * c2 : (tap + 1) * 4 * c2].astype(jnp.float32)
            down = pltpu.roll(k, 3 * c2, 1)
            up = pltpu.roll(k, c2, 1)
            blocks = [
                jnp.where(lane < c2, up, 0.0),
                jnp.where(lane < 3 * c2, down, 0.0),
                jnp.where(lane >= c2, up, 0.0),
                jnp.where(lane >= 3 * c2, down, 0.0),
            ]
            base = tap_index * 4 * c1
            for j in range(4):
                wide2[index, base + j * c1 : base + (j + 1) * c1, :] = blocks[j].astype(jnp.bfloat16)

    empty = jnp.zeros((cells, lanes), jnp.bfloat16)
    for q in range(planes2):
        hid[q, 0] = empty
        hid[q, rows2 + 1] = empty
    blank = jnp.zeros((cells, 6 * c2), jnp.bfloat16)
    for d in range(img.shape[0]):
        img[d, 0, 0] = blank
        img[d, rows2, 1] = blank

    def load(job):
        for q in range(planes2):
            pd, n = 1 - q % 2, q // 2
            pair = jnp.stack([part_refs[(pd, 0)][job, n], part_refs[(pd, 1)][job, n]], axis=1)
            hid[q, 1 : rows2 + 1] = pair.reshape(rows2, cells, lanes)

        critic = critic_ref if job == 0 else mate_critic_ref
        none = jnp.zeros((c2, c3), jnp.bfloat16)
        for tap in range(16):
            base = tap * 6 * c2
            k = [critic[(4 * tap + j) * c2 : (4 * tap + j + 1) * c2, :] for j in range(4)]
            at_left = [k[1], k[2], k[3], none, none, k[0]]
            at_right = [none, k[0], k[1], k[2], k[3], none]
            for j in range(6):
                wide3[base + j * c2 : base + (j + 1) * c2, :c3] = at_left[j]
                wide3[base + j * c2 : base + (j + 1) * c2, c3:] = at_right[j]

    def generate(index):
        pd, ph = phases[index]
        edge = 0 if pd == 1 else planes2 - 2
        inside = z > 0 if pd == 1 else z < lax.axis_size("depth") - 1

        def plane(n, carry):
            parts = [
                hid[n + td, th + ph : th + ph + rows2].reshape(rows2 * cells, lanes)
                for td, th in taps
            ]
            total = jnp.dot(
                jnp.concatenate(parts, axis=1), wide2[index], preferred_element_type=jnp.float32
            )
            total = jnp.where(jnp.logical_or(n != edge, inside), jnp.tanh(total), 0.0)
            total = total.reshape(rows2, cells, 4 * c2)
            first, second = total[:, :, : 2 * c2], total[:, :, 2 * c2 :]
            place = lax.broadcasted_iota(jnp.int32, first.shape, 1)
            column = lax.broadcasted_iota(jnp.int32, first.shape, 2)
            after = jnp.where(place == cells - 1, 0.0, pltpu.roll(first, cells - 1, 1))
            before = jnp.where(place == 0, 0.0, pltpu.roll(second, 1, 1))
            side = jnp.where(column < c2, after, before)
            result = jnp.concatenate([first, second, side], axis=2).astype(jnp.bfloat16)
            if ph == 0:
                img[2 * n + 1 - pd, 0:rows2, 1] = result
            else:
                img[2 * n + 1 - pd, 1 : rows2 + 1, 0] = result
            return carry

        lax.fori_loop(0, planes2 - 1, plane, 0)

    def judge(job):
        def plane(m, carry):
            parts = [
                img[2 * m + kd, kh // 2 : kh // 2 + rows2, kh % 2].reshape(rows2 * cells, 6 * c2)
                for kd in range(4)
                for kh in range(4)
            ]
            total = jnp.dot(
                jnp.concatenate(parts, axis=1), wide3[...], preferred_element_type=jnp.float32
            )
            total = jnp.where(total > 0, total, leak_slope * total)
            count = rows2 * cells
            stage[pl.ds(0, count, stride=2), :] = total[:, :c3]
            stage[pl.ds(1, count, stride=2), :] = total[:, c3:]
            out_ref[job, m] = stage[...].reshape(rows2, 2 * cells, c3).astype(jnp.bfloat16)
            return carry

        lax.fori_loop(0, out_planes, plane, 0)

    half = out_planes // 2

    def swap(r):
        copies = []
        for piece in (0, 1):
            span = pl.ds(piece * half, half)
            copy = pltpu.make_async_remote_copy(
                src_ref=out_ref.at[1, span],
                dst_ref=got.at[r, span],
                send_sem=send_sem.at[piece, r],
                recv_sem=recv_sem.at[piece, r],
                device_id={"trainer": peers[bits[piece][r]]},
                device_id_type=mesh_ids,
            )
            copy.start()
            copies.append(copy)
        return copies

    def settle(r, copies):
        for piece, copy in enumerate(copies):
            copy.wait()
            chosen = offset_ref[bits[piece][r]] == 1
            for m in range(piece * half, (piece + 1) * half):
                out_ref[1, m] = jnp.where(chosen, got[r, m], out_ref[1, m])

    load(1)
    for index in range(4):
        generate(index)
    judge(1)
    pl.semaphore_wait(barrier, rounds)
    moving = swap(0)
    load(0)
    settled = {(r + 1) * 4 // (rounds - 1) - 1: r for r in range(rounds - 1)}
    for index in range(4):
        generate(index)
        if index in settled:
            settle(settled[index], moving)
            moving = swap(settled[index] + 1)
    judge(0)
    settle(rounds - 1, moving)


def judged_both(offset_bits, parts, second, mate_critic, critic, bits):
    jobs, planes, rows, cells, lanes = parts[0].shape
    count = 2 * (planes - 1)
    rows2 = 2 * rows
    c2 = second.shape[1] // 64
    c1 = second.shape[0]
    c3 = critic.shape[1]
    rounds = len(bits[0])
    flops = 2 * jobs * rows2 * cells * 4 * c2 * ((count + 1) * 4 * 16 * c1 + count * 96 * c2)
    in_vmem = pl.BlockSpec(memory_space=pltpu.VMEM)
    feature_shape = (count, rows2, 2 * cells, c3)
    return pl.pallas_call(
        functools.partial(judged_kernel, bits),
        out_shape=jax.ShapeDtypeStruct((jobs,) + feature_shape, jnp.bfloat16),
        in_specs=[pl.BlockSpec(memory_space=pltpu.SMEM)] + [in_vmem] * 7,
        out_specs=in_vmem,
        scratch_shapes=[
            pltpu.VMEM((count + 2, rows2 + 2, cells, lanes), jnp.bfloat16),
            pltpu.VMEM((4, 4 * lanes, 4 * c2), jnp.bfloat16),
            pltpu.VMEM((2 * count + 2, rows2 + 1, 2, cells, 6 * c2), jnp.bfloat16),
            pltpu.VMEM((96 * c2, 2 * c3), jnp.bfloat16),
            pltpu.VMEM((rows2 * cells * 2, c3), jnp.float32),
            pltpu.VMEM((rounds,) + feature_shape, jnp.bfloat16),
            pltpu.SemaphoreType.DMA((2, rounds)),
            pltpu.SemaphoreType.DMA((2, rounds)),
        ],
        compiler_params=pltpu.CompilerParams(
            vmem_limit_bytes=budget, collective_id=1, has_side_effects=True
        ),
        cost_estimate=pl.CostEstimate(flops=flops, bytes_accessed=2**24, transcendentals=0),
        name="judged",
    )(offset_bits, *parts, second, mate_critic, critic)


def local(latent, gen_first, gen_second, critic, partner):
    trainer_index = lax.axis_index("trainer")
    offset = jnp.bitwise_xor(partner[trainer_index], trainer_index)
    rounds = lax.axis_size("trainer").bit_length() - 1
    orders = (
        tuple(range(1, rounds)) + (0,),
        tuple(range(rounds - 1, 0, -1)) + (0,),
    )
    bits = orders[0]
    offset_bits = jnp.stack([jnp.bitwise_and(jnp.right_shift(offset, b), 1) for b in range(rounds)])
    *parts, second, mate_critic = hidden_parts(
        offset_bits, latent[0], gen_first[0], gen_second[0], critic[0], bits
    )
    second = second.reshape(-1, second.shape[2])
    return judged_both(offset_bits, parts, second, mate_critic, critic[0], orders)[None]


def solution(mesh):
    in_specs = (
        P("trainer", "depth", None, None, None),
        P("trainer", "depth", None),
        P("trainer", "depth", None),
        P("trainer", None, None),
        P(),
    )
    out_specs = P("trainer", None, "depth", None, None, None)
    return jax.shard_map(local, mesh=mesh, in_specs=in_specs, out_specs=out_specs, check_vma=False)
```

```python
import functools

import jax
import jax.numpy as jnp
from jax import lax
from jax.experimental import pallas as pl
from jax.experimental.pallas import tpu as pltpu
from jax.sharding import PartitionSpec as P

leak_slope = 0.2
phases = [(pd, ph) for pd in (0, 1) for ph in (0, 1)]
taps = [(td, th) for td in (0, 1) for th in (0, 1)]
budget = 56 * 2**20
mesh_ids = pl.DeviceIdType.MESH


def hidden_kernel(
    bits, offset_ref, lat_ref, first_ref, second_ref, critic_ref,
    p00, p01, p10, p11, second_out, critic_out,
    first_all, lat_all, lat_cur, lat_got, critic_got, packed, wide, acc,
    first_send, first_recv, second_send, second_recv,
    lat_send, lat_recv, critic_send, critic_recv, halo_send, halo_recv,
):
    part_refs = (p00, p01, p10, p11)
    jobs, planes, rows, cells, lanes = p00.shape
    slab = planes - 1
    c1 = lanes // 4
    count = lax.axis_size("depth")
    z = lax.axis_index("depth")
    t = lax.axis_index("trainer")
    right, left = lax.rem(z + 1, count), lax.rem(z + count - 1, count)
    towards = (right, left)
    peers = [t + (1 << b) * (1 - 2 * lax.rem(t // (1 << b), 2)) for b in bits]
    cs = first_ref.shape[0]
    quarter = first_ref.shape[1] // 4
    last = count - 1

    barrier = pltpu.get_barrier_semaphore()
    for there in towards:
        pl.semaphore_signal(barrier, inc=1, device_id={"depth": there}, device_id_type=mesh_ids)
    for peer in peers:
        pl.semaphore_signal(barrier, inc=1, device_id={"trainer": peer}, device_id_type=mesh_ids)

    for pd, td in taps:
        for kh in range(4):
            base = (3 - pd - 2 * td) * quarter + kh * 4 * c1
            piece = first_ref[:, base : base + 4 * c1]
            first_all[z, pd, td, kh] = piece.astype(jnp.bfloat16)
    second_out[z] = second_ref[...].astype(jnp.bfloat16)
    lat_cur[...] = lat_ref[...]
    critic_out[...] = critic_ref[...]
    blank = jnp.zeros((cells, lat_ref.shape[3]), jnp.bfloat16)
    for j in range(jobs):
        for d in range(slab):
            lat_all[j, d + 1, 0] = blank
            lat_all[j, d + 1, rows + 1] = blank
    for d in range(slab):
        lat_all[0, d + 1, 1 : rows + 1] = lat_ref[d]
    pl.semaphore_wait(barrier, 2 + len(bits))

    def sent(src, dst, send, recv, **where):
        copy = pltpu.make_async_remote_copy(
            src_ref=src, dst_ref=dst, send_sem=send, recv_sem=recv,
            device_id=where, device_id_type=mesh_ids,
        )
        copy.start()
        return copy

    def halo(job, way):
        src, dst = ((slab, 0), (1, slab + 1))[way]
        return pltpu.make_async_remote_copy(
            src_ref=lat_all.at[job, src], dst_ref=lat_all.at[job, dst],
            send_sem=halo_send.at[job, way], recv_sem=halo_recv.at[job, way],
            device_id={"depth": towards[way]}, device_id_type=mesh_ids,
        )

    def owner_of(way, step):
        return lax.rem(z + count - step, count) if way == 0 else lax.rem(z + step, count)

    def sends(way, step):
        if way == 0:
            return jnp.logical_and(z < last, z >= step - 1)
        return jnp.logical_and(z > 0, z + step - 1 <= last)

    def receives(way, step):
        return z >= step if way == 0 else z + step <= last

    def first_hop(way, step, owner, pd, td):
        return pltpu.make_async_remote_copy(
            src_ref=first_all.at[owner, pd, td], dst_ref=first_all.at[owner, pd, td],
            send_sem=first_send.at[way, step - 1, pd, td],
            recv_sem=first_recv.at[way, step - 1, pd, td],
            device_id={"depth": towards[way]}, device_id_type=mesh_ids,
        )

    def second_hop(way, step, owner):
        return pltpu.make_async_remote_copy(
            src_ref=second_out.at[owner], dst_ref=second_out.at[owner],
            send_sem=second_send.at[way, step - 1], recv_sem=second_recv.at[way, step - 1],
            device_id={"depth": towards[way]}, device_id_type=mesh_ids,
        )

    def pass_first(step):
        for pd, td in taps:
            for way in (0, 1):
                if step > 1:
                    @pl.when(receives(way, step - 1))
                    def _():
                        first_hop(way, step - 1, owner_of(way, step - 1), pd, td).wait_recv()
                if step < count:
                    @pl.when(sends(way, step))
                    def _():
                        first_hop(way, step, owner_of(way, step - 1), pd, td).start()

    def pass_second(step):
        for way in (0, 1):
            if step > 1:
                @pl.when(receives(way, step - 1))
                def _():
                    second_hop(way, step - 1, owner_of(way, step - 1)).wait_recv()
            if step < count:
                @pl.when(sends(way, step))
                def _():
                    second_hop(way, step, owner_of(way, step - 1)).start()

    def swap_latent(r):
        return sent(lat_cur, lat_got.at[r], lat_send.at[r], lat_recv.at[r], trainer=peers[r])

    def swap_critic(r):
        return sent(critic_out, critic_got.at[r], critic_send.at[r], critic_recv.at[r],
                    trainer=peers[r])

    def chosen(r):
        return offset_ref[bits[r]] == 1

    def start_halos(job):
        for way in (0, 1):
            @pl.when(sends(way, 1))
            def _():
                halo(job, way).start()

    moving = swap_latent(0)
    start_halos(0)
    pass_first(1)
    for r in range(len(bits)):
        moving.wait()
        lat_cur[...] = jnp.where(chosen(r), lat_got[r], lat_cur[...])
        if r + 1 < len(bits):
            moving = swap_latent(r + 1)
    for d in range(slab):
        lat_all[1, d + 1, 1 : rows + 1] = lat_cur[d]
    start_halos(1)
    critic_move = swap_critic(0)
    for way in (0, 1):
        end = (0, slab + 1)[way]
        for job in range(jobs):
            @pl.when(receives(way, 1))
            def _():
                halo(job, way).wait_recv()

            @pl.when(jnp.logical_not(receives(way, 1)))
            def _():
                lat_all[job, end] = jnp.zeros(lat_all.shape[2:], jnp.bfloat16)

    per = 128 // cs
    group_rows = jobs * (rows + 1)

    def pack(n, carry):
        for s in range(count):
            tile, off = s * cs // 128 * 128, s * cs % 128
            for g in range(4 // per):
                center = None
                for i in range(per):
                    td, th = divmod(g * per + i, 2)
                    x = lat_all[:, n + td, th : th + rows + 1, :, tile : tile + 128]
                    x = x.astype(jnp.float32).reshape(group_rows * cells, 128)
                    shift = (i * cs - off) % 128
                    x = pltpu.roll(x, shift, 1) if shift else x
                    lane = lax.broadcasted_iota(jnp.int32, x.shape, 1)
                    center = x if center is None else jnp.where(lane < i * cs, center, x)
                center = center.reshape(group_rows, cells, 128)
                place = lax.broadcasted_iota(jnp.int32, center.shape, 1)
                before = jnp.where(place == 0, 0.0, pltpu.roll(center, 1, 1))
                after = jnp.where(place == cells - 1, 0.0, pltpu.roll(center, cells - 1, 1))
                for j, value in enumerate((before, center, after)):
                    base = j * 4 * cs + g * 128
                    packed[s, :, n, :, :, base : base + 128] = value.astype(jnp.bfloat16).reshape(
                        jobs, rows + 1, cells, 128
                    )
        return carry

    lax.fori_loop(0, planes, pack, 0)

    none = jnp.zeros((cs, c1), jnp.bfloat16)

    def add_shard(owner, start):
        def phase(index, carry):
            pd, ph = index // 2, lax.rem(index, 2)
            for td, th in taps:
                block = first_all.at[owner, pd, td, 3 - ph - 2 * th]
                k = [block[:, j * c1 : (j + 1) * c1] for j in range(4)]
                for j, (a, b) in enumerate(((k[3], none), (k[1], k[2]), (none, k[0]))):
                    base = (4 * j + 2 * td + th) * cs
                    wide[base : base + cs, :c1] = a
                    wide[base : base + cs, c1:] = b

            def plane(n, inner):
                lhs = packed[owner, :, n, pl.ds(ph, rows)].reshape(jobs * rows * cells, 12 * cs)
                total = jnp.dot(lhs, wide[...], preferred_element_type=jnp.float32)
                acc[index, n] = total if start else acc[index, n] + total
                return inner

            return lax.fori_loop(0, planes, plane, carry)

        lax.fori_loop(0, 4, phase, 0)

    for step in range(count):
        if step:
            pass_first(step + 1)
        if step == min(2, last):
            pass_second(1)
        if step == 0:
            add_shard(z, True)
        else:
            for way in (0, 1):
                @pl.when(receives(way, step))
                def _():
                    add_shard(owner_of(way, step), False)
        if step < len(bits):
            critic_move.wait()
            critic_out[...] = jnp.where(chosen(step), critic_got[step], critic_out[...])
            if step + 1 < len(bits):
                critic_move = swap_critic(step + 1)

    pass_second(2)
    for index, (pd, ph) in enumerate(phases):
        edge = 0 if pd == 1 else planes - 1
        inside = z > 0 if pd == 1 else z < count - 1

        def finish(n, carry, index=index, edge=edge, inside=inside):
            keep = jnp.logical_or(n != edge, inside)
            total = jnp.where(keep, jnp.maximum(acc[index, n], 0.0), 0.0)
            total = total.reshape(jobs * rows, cells, 2 * c1)
            even, odd = total[:, :, :c1], total[:, :, c1:]
            place = lax.broadcasted_iota(jnp.int32, even.shape, 1)
            before = jnp.where(place == 0, 0.0, pltpu.roll(odd, 1, 1))
            after = jnp.where(place == cells - 1, 0.0, pltpu.roll(even, cells - 1, 1))
            result = jnp.concatenate([before, even, odd, after], axis=2).astype(jnp.bfloat16)
            part_refs[index][:, n] = result.reshape(jobs, rows, cells, lanes)
            return carry

        lax.fori_loop(0, planes, finish, 0)
        if index == 1:
            pass_second(3)

    for step in range(4, count + 1):
        pass_second(step)
    for way in (0, 1):
        for step in range(1, count):
            @pl.when(sends(way, step))
            def _():
                for pd, td in taps:
                    first_hop(way, step, owner_of(way, step - 1), pd, td).wait_send()
                second_hop(way, step, owner_of(way, step - 1)).wait_send()

        @pl.when(sends(way, 1))
        def _():
            for job in range(jobs):
                halo(job, way).wait_send()


def hidden_parts(offset_bits, latent, first, second, critic, bits):
    slab, rows, cells, c0 = latent.shape
    count = lax.axis_size("depth")
    cs, columns = first.shape
    c1 = columns // 64
    rounds = len(bits)
    part = jax.ShapeDtypeStruct((2, slab + 1, rows, cells, 4 * c1), jnp.bfloat16)
    in_vmem = pl.BlockSpec(memory_space=pltpu.VMEM)
    dma = pltpu.SemaphoreType.DMA
    flops = 2 * 2 * (slab + 1) * rows * cells * 4 * 12 * c0 * 2 * c1
    return pl.pallas_call(
        functools.partial(hidden_kernel, bits),
        out_shape=[part] * 4
        + [
            jax.ShapeDtypeStruct((count,) + second.shape, jnp.bfloat16),
            jax.ShapeDtypeStruct(critic.shape, jnp.bfloat16),
        ],
        in_specs=[pl.BlockSpec(memory_space=pltpu.SMEM)] + [in_vmem] * 4,
        out_specs=[in_vmem] * 6,
        scratch_shapes=[
            pltpu.VMEM((count, 2, 2, 4, cs, columns // 16), jnp.bfloat16),
            pltpu.VMEM((2, slab + 2, rows + 2, cells, c0), jnp.bfloat16),
            pltpu.VMEM(latent.shape, jnp.bfloat16),
            pltpu.VMEM((rounds,) + latent.shape, jnp.bfloat16),
            pltpu.VMEM((rounds,) + critic.shape, jnp.bfloat16),
            pltpu.VMEM((count, 2, slab + 1, rows + 1, cells, 12 * cs), jnp.bfloat16),
            pltpu.VMEM((12 * cs, 2 * c1), jnp.bfloat16),
            pltpu.VMEM((4, slab + 1, 2 * rows * cells, 2 * c1), jnp.float32),
            dma((2, count - 1, 2, 2)),
            dma((2, count - 1, 2, 2)),
            dma((2, count - 1)),
            dma((2, count - 1)),
            dma((rounds,)),
            dma((rounds,)),
            dma((rounds,)),
            dma((rounds,)),
            dma((2, 2)),
            dma((2, 2)),
        ],
        compiler_params=pltpu.CompilerParams(
            vmem_limit_bytes=budget, collective_id=0, has_side_effects=True
        ),
        cost_estimate=pl.CostEstimate(flops=flops, bytes_accessed=2**24, transcendentals=0),
        name="hidden",
    )(offset_bits, latent, first, second, critic)


def judged_kernel(
    bits, offset_ref, p00, p01, p10, p11, w_ref, mate_critic_ref, critic_ref, out_ref,
    hid, wide2, img, wide3, stage, got, send_sem, recv_sem,
):
    part_refs = {(0, 0): p00, (0, 1): p01, (1, 0): p10, (1, 1): p11}
    planes2, rows2, cells, lanes = hid.shape
    rows2 = rows2 - 2
    c1 = lanes // 4
    c2 = c1 // 2
    out_planes, c3 = out_ref.shape[1], out_ref.shape[4]
    z = lax.axis_index("depth")
    t = lax.axis_index("trainer")
    rounds = len(bits[0])
    peers = [t + (1 << b) * (1 - 2 * lax.rem(t // (1 << b), 2)) for b in range(rounds)]
    barrier = pltpu.get_barrier_semaphore()
    for peer in peers:
        pl.semaphore_signal(barrier, inc=1, device_id={"trainer": peer}, device_id_type=mesh_ids)

    lane = lax.broadcasted_iota(jnp.int32, (c1, 4 * c2), 1)
    for index, (pd, ph) in enumerate(phases):
        for tap_index, (td, th) in enumerate(taps):
            tap = (3 - pd - 2 * td) * 4 + 3 - ph - 2 * th
            k = w_ref[:, tap * 4 * c2 : (tap + 1) * 4 * c2].astype(jnp.float32)
            down = pltpu.roll(k, 3 * c2, 1)
            up = pltpu.roll(k, c2, 1)
            blocks = [
                jnp.where(lane < c2, up, 0.0),
                jnp.where(lane < 3 * c2, down, 0.0),
                jnp.where(lane >= c2, up, 0.0),
                jnp.where(lane >= 3 * c2, down, 0.0),
            ]
            base = tap_index * 4 * c1
            for j in range(4):
                wide2[index, base + j * c1 : base + (j + 1) * c1, :] = blocks[j].astype(jnp.bfloat16)

    empty = jnp.zeros((cells, lanes), jnp.bfloat16)
    for q in range(planes2):
        hid[q, 0] = empty
        hid[q, rows2 + 1] = empty
    blank = jnp.zeros((cells, 6 * c2), jnp.bfloat16)
    for d in range(img.shape[0]):
        img[d, 0, 0] = blank
        img[d, rows2, 1] = blank

    def load(job):
        for q in range(planes2):
            pd, n = 1 - q % 2, q // 2
            pair = jnp.stack([part_refs[(pd, 0)][job, n], part_refs[(pd, 1)][job, n]], axis=1)
            hid[q, 1 : rows2 + 1] = pair.reshape(rows2, cells, lanes)

        critic = critic_ref if job == 0 else mate_critic_ref
        none = jnp.zeros((c2, c3), jnp.bfloat16)
        for tap in range(16):
            base = tap * 6 * c2
            k = [critic[(4 * tap + j) * c2 : (4 * tap + j + 1) * c2, :] for j in range(4)]
            at_left = [k[1], k[2], k[3], none, none, k[0]]
            at_right = [none, k[0], k[1], k[2], k[3], none]
            for j in range(6):
                wide3[base + j * c2 : base + (j + 1) * c2, :c3] = at_left[j]
                wide3[base + j * c2 : base + (j + 1) * c2, c3:] = at_right[j]

    def generate(index):
        pd, ph = phases[index]
        edge = 0 if pd == 1 else planes2 - 2
        inside = z > 0 if pd == 1 else z < lax.axis_size("depth") - 1

        def plane(n, carry):
            parts = [
                hid[n + td, th + ph : th + ph + rows2].reshape(rows2 * cells, lanes)
                for td, th in taps
            ]
            total = jnp.dot(
                jnp.concatenate(parts, axis=1), wide2[index], preferred_element_type=jnp.float32
            )
            total = jnp.where(jnp.logical_or(n != edge, inside), jnp.tanh(total), 0.0)
            total = total.reshape(rows2, cells, 4 * c2)
            first, second = total[:, :, : 2 * c2], total[:, :, 2 * c2 :]
            place = lax.broadcasted_iota(jnp.int32, first.shape, 1)
            column = lax.broadcasted_iota(jnp.int32, first.shape, 2)
            after = jnp.where(place == cells - 1, 0.0, pltpu.roll(first, cells - 1, 1))
            before = jnp.where(place == 0, 0.0, pltpu.roll(second, 1, 1))
            side = jnp.where(column < c2, after, before)
            result = jnp.concatenate([first, second, side], axis=2).astype(jnp.bfloat16)
            if ph == 0:
                img[2 * n + 1 - pd, 0:rows2, 1] = result
            else:
                img[2 * n + 1 - pd, 1 : rows2 + 1, 0] = result
            return carry

        lax.fori_loop(0, planes2 - 1, plane, 0)

    def judge(job):
        def plane(m, carry):
            parts = [
                img[2 * m + kd, kh // 2 : kh // 2 + rows2, kh % 2].reshape(rows2 * cells, 6 * c2)
                for kd in range(4)
                for kh in range(4)
            ]
            total = jnp.dot(
                jnp.concatenate(parts, axis=1), wide3[...], preferred_element_type=jnp.float32
            )
            total = jnp.where(total > 0, total, leak_slope * total)
            count = rows2 * cells
            stage[pl.ds(0, count, stride=2), :] = total[:, :c3]
            stage[pl.ds(1, count, stride=2), :] = total[:, c3:]
            out_ref[job, m] = stage[...].reshape(rows2, 2 * cells, c3).astype(jnp.bfloat16)
            return carry

        lax.fori_loop(0, out_planes, plane, 0)

    half = out_planes // 2

    def swap(r):
        copies = []
        for piece in (0, 1):
            span = pl.ds(piece * half, half)
            copy = pltpu.make_async_remote_copy(
                src_ref=out_ref.at[1, span],
                dst_ref=got.at[r, span],
                send_sem=send_sem.at[piece, r],
                recv_sem=recv_sem.at[piece, r],
                device_id={"trainer": peers[bits[piece][r]]},
                device_id_type=mesh_ids,
            )
            copy.start()
            copies.append(copy)
        return copies

    def settle(r, copies):
        for piece, copy in enumerate(copies):
            copy.wait()
            chosen = offset_ref[bits[piece][r]] == 1
            for m in range(piece * half, (piece + 1) * half):
                out_ref[1, m] = jnp.where(chosen, got[r, m], out_ref[1, m])

    load(1)
    for index in range(4):
        generate(index)
    judge(1)
    pl.semaphore_wait(barrier, rounds)
    moving = swap(0)
    load(0)
    settled = {(r + 1) * 4 // (rounds - 1) - 1: r for r in range(rounds - 1)}
    for index in range(4):
        generate(index)
        if index in settled:
            settle(settled[index], moving)
            moving = swap(settled[index] + 1)
    judge(0)
    settle(rounds - 1, moving)


def judged_both(offset_bits, parts, second, mate_critic, critic, bits):
    jobs, planes, rows, cells, lanes = parts[0].shape
    count = 2 * (planes - 1)
    rows2 = 2 * rows
    c2 = second.shape[1] // 64
    c1 = second.shape[0]
    c3 = critic.shape[1]
    rounds = len(bits[0])
    flops = 2 * jobs * rows2 * cells * 4 * c2 * ((count + 1) * 4 * 16 * c1 + count * 96 * c2)
    in_vmem = pl.BlockSpec(memory_space=pltpu.VMEM)
    feature_shape = (count, rows2, 2 * cells, c3)
    return pl.pallas_call(
        functools.partial(judged_kernel, bits),
        out_shape=jax.ShapeDtypeStruct((jobs,) + feature_shape, jnp.bfloat16),
        in_specs=[pl.BlockSpec(memory_space=pltpu.SMEM)] + [in_vmem] * 7,
        out_specs=in_vmem,
        scratch_shapes=[
            pltpu.VMEM((count + 2, rows2 + 2, cells, lanes), jnp.bfloat16),
            pltpu.VMEM((4, 4 * lanes, 4 * c2), jnp.bfloat16),
            pltpu.VMEM((2 * count + 2, rows2 + 1, 2, cells, 6 * c2), jnp.bfloat16),
            pltpu.VMEM((96 * c2, 2 * c3), jnp.bfloat16),
            pltpu.VMEM((rows2 * cells * 2, c3), jnp.float32),
            pltpu.VMEM((rounds,) + feature_shape, jnp.bfloat16),
            pltpu.SemaphoreType.DMA((2, rounds)),
            pltpu.SemaphoreType.DMA((2, rounds)),
        ],
        compiler_params=pltpu.CompilerParams(
            vmem_limit_bytes=budget, collective_id=1, has_side_effects=True
        ),
        cost_estimate=pl.CostEstimate(flops=flops, bytes_accessed=2**24, transcendentals=0),
        name="judged",
    )(offset_bits, *parts, second, mate_critic, critic)


def local(latent, gen_first, gen_second, critic, partner):
    trainer_index = lax.axis_index("trainer")
    offset = jnp.bitwise_xor(partner[trainer_index], trainer_index)
    rounds = lax.axis_size("trainer").bit_length() - 1
    orders = (
        tuple(range(1, rounds)) + (0,),
        tuple(range(rounds - 1, 0, -1)) + (0,),
    )
    bits = orders[0]
    offset_bits = jnp.stack([jnp.bitwise_and(jnp.right_shift(offset, b), 1) for b in range(rounds)])
    *parts, second, mate_critic = hidden_parts(
        offset_bits, latent[0], gen_first[0], gen_second[0], critic[0], bits
    )
    second = second.reshape(-1, second.shape[2])
    return judged_both(offset_bits, parts, second, mate_critic, critic[0], orders)[None]


def solution(mesh):
    in_specs = (
        P("trainer", "depth", None, None, None),
        P("trainer", "depth", None),
        P("trainer", "depth", None),
        P("trainer", None, None),
        P(),
    )
    out_specs = P("trainer", None, "depth", None, None, None)
    return jax.shard_map(local, mesh=mesh, in_specs=in_specs, out_specs=out_specs, check_vma=False)
```

```python
import functools

import jax
import jax.numpy as jnp
from jax import lax
from jax.experimental import pallas as pl
from jax.experimental.pallas import tpu as pltpu
from jax.sharding import PartitionSpec as P

leak_slope = 0.2
phases = [(pd, ph) for pd in (0, 1) for ph in (0, 1)]
taps = [(td, th) for td in (0, 1) for th in (0, 1)]
budget = 56 * 2**20
mesh_ids = pl.DeviceIdType.MESH


def hidden_kernel(
    bits, partner_ref, lat_ref, first_ref, second_ref, critic_ref,
    p00, p01, p10, p11, second_out, critic_out,
    first_all, lat_all, lat_cur, lat_got, critic_got, packed, wide, acc,
    first_send, first_recv, second_send, second_recv,
    lat_send, lat_recv, critic_send, critic_recv, halo_send, halo_recv,
):
    part_refs = (p00, p01, p10, p11)
    jobs, planes, rows, cells, lanes = p00.shape
    slab = planes - 1
    c1 = lanes // 4
    count = lax.axis_size("depth")
    z = lax.axis_index("depth")
    t = lax.axis_index("trainer")
    right, left = lax.rem(z + 1, count), lax.rem(z + count - 1, count)
    towards = (right, left)
    peers = [t + (1 << b) * (1 - 2 * lax.rem(t // (1 << b), 2)) for b in bits]
    cs = first_ref.shape[0]
    quarter = first_ref.shape[1] // 4
    last = count - 1

    barrier = pltpu.get_barrier_semaphore()
    for there in towards:
        pl.semaphore_signal(barrier, inc=1, device_id={"depth": there}, device_id_type=mesh_ids)
    for peer in peers:
        pl.semaphore_signal(barrier, inc=1, device_id={"trainer": peer}, device_id_type=mesh_ids)

    for pd, td in taps:
        for kh in range(4):
            base = (3 - pd - 2 * td) * quarter + kh * 4 * c1
            piece = first_ref[:, base : base + 4 * c1]
            first_all[z, pd, td, kh] = piece.astype(jnp.bfloat16)
    second_out[z] = second_ref[...].astype(jnp.bfloat16)
    lat_cur[...] = lat_ref[...]
    critic_out[...] = critic_ref[...]
    blank = jnp.zeros((cells, lat_ref.shape[3]), jnp.bfloat16)
    for j in range(jobs):
        for d in range(slab):
            lat_all[j, d + 1, 0] = blank
            lat_all[j, d + 1, rows + 1] = blank
    for d in range(slab):
        lat_all[0, d + 1, 1 : rows + 1] = lat_ref[d]
    pl.semaphore_wait(barrier, 2 + len(bits))

    def sent(src, dst, send, recv, **where):
        copy = pltpu.make_async_remote_copy(
            src_ref=src, dst_ref=dst, send_sem=send, recv_sem=recv,
            device_id=where, device_id_type=mesh_ids,
        )
        copy.start()
        return copy

    def halo(job, way):
        src, dst = ((slab, 0), (1, slab + 1))[way]
        return pltpu.make_async_remote_copy(
            src_ref=lat_all.at[job, src], dst_ref=lat_all.at[job, dst],
            send_sem=halo_send.at[job, way], recv_sem=halo_recv.at[job, way],
            device_id={"depth": towards[way]}, device_id_type=mesh_ids,
        )

    def owner_of(way, step):
        return lax.rem(z + count - step, count) if way == 0 else lax.rem(z + step, count)

    def sends(way, step):
        if way == 0:
            return jnp.logical_and(z < last, z >= step - 1)
        return jnp.logical_and(z > 0, z + step - 1 <= last)

    def receives(way, step):
        return z >= step if way == 0 else z + step <= last

    def first_hop(way, step, owner, pd, td):
        return pltpu.make_async_remote_copy(
            src_ref=first_all.at[owner, pd, td], dst_ref=first_all.at[owner, pd, td],
            send_sem=first_send.at[way, step - 1, pd, td],
            recv_sem=first_recv.at[way, step - 1, pd, td],
            device_id={"depth": towards[way]}, device_id_type=mesh_ids,
        )

    def second_hop(way, step, owner):
        return pltpu.make_async_remote_copy(
            src_ref=second_out.at[owner], dst_ref=second_out.at[owner],
            send_sem=second_send.at[way, step - 1], recv_sem=second_recv.at[way, step - 1],
            device_id={"depth": towards[way]}, device_id_type=mesh_ids,
        )

    def pass_first(step):
        for pd, td in taps:
            for way in (0, 1):
                if step > 1:
                    @pl.when(receives(way, step - 1))
                    def _():
                        first_hop(way, step - 1, owner_of(way, step - 1), pd, td).wait_recv()
                if step < count:
                    @pl.when(sends(way, step))
                    def _():
                        first_hop(way, step, owner_of(way, step - 1), pd, td).start()

    def pass_second(step):
        for way in (0, 1):
            if step > 1:
                @pl.when(receives(way, step - 1))
                def _():
                    second_hop(way, step - 1, owner_of(way, step - 1)).wait_recv()
            if step < count:
                @pl.when(sends(way, step))
                def _():
                    second_hop(way, step, owner_of(way, step - 1)).start()

    def swap_latent(r):
        return sent(lat_cur, lat_got.at[r], lat_send.at[r], lat_recv.at[r], trainer=peers[r])

    def swap_critic(r):
        return sent(critic_out, critic_got.at[r], critic_send.at[r], critic_recv.at[r],
                    trainer=peers[r])

    def chosen(r):
        return jnp.bitwise_and(jnp.right_shift(partner_ref[0], bits[r]), 1) == 1

    def start_halos(job):
        for way in (0, 1):
            @pl.when(sends(way, 1))
            def _():
                halo(job, way).start()

    moving = swap_latent(0)
    start_halos(0)
    pass_first(1)
    for r in range(len(bits)):
        moving.wait()
        lat_cur[...] = jnp.where(chosen(r), lat_got[r], lat_cur[...])
        if r + 1 < len(bits):
            moving = swap_latent(r + 1)
    for d in range(slab):
        lat_all[1, d + 1, 1 : rows + 1] = lat_cur[d]
    start_halos(1)
    critic_move = swap_critic(0)
    for way in (0, 1):
        end = (0, slab + 1)[way]
        for job in range(jobs):
            @pl.when(receives(way, 1))
            def _():
                halo(job, way).wait_recv()

            @pl.when(jnp.logical_not(receives(way, 1)))
            def _():
                lat_all[job, end] = jnp.zeros(lat_all.shape[2:], jnp.bfloat16)

    per = 128 // cs
    group_rows = jobs * (rows + 1)

    def pack(n, carry):
        for s in range(count):
            tile, off = s * cs // 128 * 128, s * cs % 128
            for g in range(4 // per):
                center = None
                for i in range(per):
                    td, th = divmod(g * per + i, 2)
                    x = lat_all[:, n + td, th : th + rows + 1, :, tile : tile + 128]
                    x = x.astype(jnp.float32).reshape(group_rows * cells, 128)
                    shift = (i * cs - off) % 128
                    x = pltpu.roll(x, shift, 1) if shift else x
                    lane = lax.broadcasted_iota(jnp.int32, x.shape, 1)
                    center = x if center is None else jnp.where(lane < i * cs, center, x)
                center = center.reshape(group_rows, cells, 128)
                place = lax.broadcasted_iota(jnp.int32, center.shape, 1)
                before = jnp.where(place == 0, 0.0, pltpu.roll(center, 1, 1))
                after = jnp.where(place == cells - 1, 0.0, pltpu.roll(center, cells - 1, 1))
                for j, value in enumerate((before, center, after)):
                    base = j * 4 * cs + g * 128
                    packed[s, :, n, :, :, base : base + 128] = value.astype(jnp.bfloat16).reshape(
                        jobs, rows + 1, cells, 128
                    )
        return carry

    lax.fori_loop(0, planes, pack, 0)

    none = jnp.zeros((cs, c1), jnp.bfloat16)

    def add_shard(owner, start):
        def phase(index, carry):
            pd, ph = index // 2, lax.rem(index, 2)
            for td, th in taps:
                block = first_all.at[owner, pd, td, 3 - ph - 2 * th]
                k = [block[:, j * c1 : (j + 1) * c1] for j in range(4)]
                for j, (a, b) in enumerate(((k[3], none), (k[1], k[2]), (none, k[0]))):
                    base = (4 * j + 2 * td + th) * cs
                    wide[base : base + cs, :c1] = a
                    wide[base : base + cs, c1:] = b

            def plane(n, inner):
                lhs = packed[owner, :, n, pl.ds(ph, rows)].reshape(jobs * rows * cells, 12 * cs)
                total = jnp.dot(lhs, wide[...], preferred_element_type=jnp.float32)
                acc[index, n] = total if start else acc[index, n] + total
                return inner

            return lax.fori_loop(0, planes, plane, carry)

        lax.fori_loop(0, 4, phase, 0)

    for step in range(count):
        if step:
            pass_first(step + 1)
        if step == min(2, last):
            pass_second(1)
        if step == 0:
            add_shard(z, True)
        else:
            for way in (0, 1):
                @pl.when(receives(way, step))
                def _():
                    add_shard(owner_of(way, step), False)
        if step < len(bits):
            critic_move.wait()
            critic_out[...] = jnp.where(chosen(step), critic_got[step], critic_out[...])
            if step + 1 < len(bits):
                critic_move = swap_critic(step + 1)

    pass_second(2)
    for index, (pd, ph) in enumerate(phases):
        edge = 0 if pd == 1 else planes - 1
        inside = z > 0 if pd == 1 else z < count - 1

        def finish(n, carry, index=index, edge=edge, inside=inside):
            keep = jnp.logical_or(n != edge, inside)
            total = jnp.where(keep, jnp.maximum(acc[index, n], 0.0), 0.0)
            total = total.reshape(jobs * rows, cells, 2 * c1)
            even, odd = total[:, :, :c1], total[:, :, c1:]
            place = lax.broadcasted_iota(jnp.int32, even.shape, 1)
            before = jnp.where(place == 0, 0.0, pltpu.roll(odd, 1, 1))
            after = jnp.where(place == cells - 1, 0.0, pltpu.roll(even, cells - 1, 1))
            result = jnp.concatenate([before, even, odd, after], axis=2).astype(jnp.bfloat16)
            part_refs[index][:, n] = result.reshape(jobs, rows, cells, lanes)
            return carry

        lax.fori_loop(0, planes, finish, 0)
        if index == 1:
            pass_second(3)

    for step in range(4, count + 1):
        pass_second(step)
    for way in (0, 1):
        for step in range(1, count):
            @pl.when(sends(way, step))
            def _():
                for pd, td in taps:
                    first_hop(way, step, owner_of(way, step - 1), pd, td).wait_send()
                second_hop(way, step, owner_of(way, step - 1)).wait_send()

        @pl.when(sends(way, 1))
        def _():
            for job in range(jobs):
                halo(job, way).wait_send()


def hidden_parts(partner, latent, first, second, critic, bits):
    slab, rows, cells, c0 = latent.shape
    count = lax.axis_size("depth")
    cs, columns = first.shape
    c1 = columns // 64
    rounds = len(bits)
    part = jax.ShapeDtypeStruct((2, slab + 1, rows, cells, 4 * c1), jnp.bfloat16)
    in_vmem = pl.BlockSpec(memory_space=pltpu.VMEM)
    dma = pltpu.SemaphoreType.DMA
    flops = 2 * 2 * (slab + 1) * rows * cells * 4 * 12 * c0 * 2 * c1
    return pl.pallas_call(
        functools.partial(hidden_kernel, bits),
        out_shape=[part] * 4
        + [
            jax.ShapeDtypeStruct((count,) + second.shape, jnp.bfloat16),
            jax.ShapeDtypeStruct(critic.shape, jnp.bfloat16),
        ],
        in_specs=[pl.BlockSpec(memory_space=pltpu.SMEM)] + [in_vmem] * 4,
        out_specs=[in_vmem] * 6,
        scratch_shapes=[
            pltpu.VMEM((count, 2, 2, 4, cs, columns // 16), jnp.bfloat16),
            pltpu.VMEM((2, slab + 2, rows + 2, cells, c0), jnp.bfloat16),
            pltpu.VMEM(latent.shape, jnp.bfloat16),
            pltpu.VMEM((rounds,) + latent.shape, jnp.bfloat16),
            pltpu.VMEM((rounds,) + critic.shape, jnp.bfloat16),
            pltpu.VMEM((count, 2, slab + 1, rows + 1, cells, 12 * cs), jnp.bfloat16),
            pltpu.VMEM((12 * cs, 2 * c1), jnp.bfloat16),
            pltpu.VMEM((4, slab + 1, 2 * rows * cells, 2 * c1), jnp.float32),
            dma((2, count - 1, 2, 2)),
            dma((2, count - 1, 2, 2)),
            dma((2, count - 1)),
            dma((2, count - 1)),
            dma((rounds,)),
            dma((rounds,)),
            dma((rounds,)),
            dma((rounds,)),
            dma((2, 2)),
            dma((2, 2)),
        ],
        compiler_params=pltpu.CompilerParams(
            vmem_limit_bytes=budget, collective_id=0, has_side_effects=True
        ),
        cost_estimate=pl.CostEstimate(flops=flops, bytes_accessed=2**24, transcendentals=0),
        name="hidden",
    )(partner, latent, first, second, critic)


def judged_kernel(
    bits, partner_ref, p00, p01, p10, p11, w_ref, mate_critic_ref, critic_ref, out_ref,
    hid, wide2, img, wide3, stage, got, send_sem, recv_sem,
):
    part_refs = {(0, 0): p00, (0, 1): p01, (1, 0): p10, (1, 1): p11}
    planes2, rows2, cells, lanes = hid.shape
    rows2 = rows2 - 2
    c1 = lanes // 4
    c2 = c1 // 2
    out_planes, c3 = out_ref.shape[1], out_ref.shape[4]
    z = lax.axis_index("depth")
    t = lax.axis_index("trainer")
    rounds = len(bits[0])
    peers = [t + (1 << b) * (1 - 2 * lax.rem(t // (1 << b), 2)) for b in range(rounds)]
    barrier = pltpu.get_barrier_semaphore()
    for peer in peers:
        pl.semaphore_signal(barrier, inc=1, device_id={"trainer": peer}, device_id_type=mesh_ids)

    lane = lax.broadcasted_iota(jnp.int32, (c1, 4 * c2), 1)
    for index, (pd, ph) in enumerate(phases):
        for tap_index, (td, th) in enumerate(taps):
            tap = (3 - pd - 2 * td) * 4 + 3 - ph - 2 * th
            k = w_ref[:, tap * 4 * c2 : (tap + 1) * 4 * c2].astype(jnp.float32)
            down = pltpu.roll(k, 3 * c2, 1)
            up = pltpu.roll(k, c2, 1)
            blocks = [
                jnp.where(lane < c2, up, 0.0),
                jnp.where(lane < 3 * c2, down, 0.0),
                jnp.where(lane >= c2, up, 0.0),
                jnp.where(lane >= 3 * c2, down, 0.0),
            ]
            base = tap_index * 4 * c1
            for j in range(4):
                wide2[index, base + j * c1 : base + (j + 1) * c1, :] = blocks[j].astype(jnp.bfloat16)

    empty = jnp.zeros((cells, lanes), jnp.bfloat16)
    for q in range(planes2):
        hid[q, 0] = empty
        hid[q, rows2 + 1] = empty
    blank = jnp.zeros((cells, 6 * c2), jnp.bfloat16)
    for d in range(img.shape[0]):
        img[d, 0, 0] = blank
        img[d, rows2, 1] = blank

    def load(job):
        for q in range(planes2):
            pd, n = 1 - q % 2, q // 2
            pair = jnp.stack([part_refs[(pd, 0)][job, n], part_refs[(pd, 1)][job, n]], axis=1)
            hid[q, 1 : rows2 + 1] = pair.reshape(rows2, cells, lanes)

        critic = critic_ref if job == 0 else mate_critic_ref
        none = jnp.zeros((c2, c3), jnp.bfloat16)
        for tap in range(16):
            base = tap * 6 * c2
            k = [critic[(4 * tap + j) * c2 : (4 * tap + j + 1) * c2, :] for j in range(4)]
            at_left = [k[1], k[2], k[3], none, none, k[0]]
            at_right = [none, k[0], k[1], k[2], k[3], none]
            for j in range(6):
                wide3[base + j * c2 : base + (j + 1) * c2, :c3] = at_left[j]
                wide3[base + j * c2 : base + (j + 1) * c2, c3:] = at_right[j]

    def generate(index):
        pd, ph = phases[index]
        edge = 0 if pd == 1 else planes2 - 2
        inside = z > 0 if pd == 1 else z < lax.axis_size("depth") - 1

        def plane(n, carry):
            parts = [
                hid[n + td, th + ph : th + ph + rows2].reshape(rows2 * cells, lanes)
                for td, th in taps
            ]
            total = jnp.dot(
                jnp.concatenate(parts, axis=1), wide2[index], preferred_element_type=jnp.float32
            )
            total = jnp.tanh(total)
            total = total.reshape(rows2, cells, 4 * c2)
            first, second = total[:, :, : 2 * c2], total[:, :, 2 * c2 :]
            place = lax.broadcasted_iota(jnp.int32, first.shape, 1)
            column = lax.broadcasted_iota(jnp.int32, first.shape, 2)
            after = jnp.where(place == cells - 1, 0.0, pltpu.roll(first, cells - 1, 1))
            before = jnp.where(place == 0, 0.0, pltpu.roll(second, 1, 1))
            side = jnp.where(column < c2, after, before)
            result = jnp.concatenate([first, second, side], axis=2).astype(jnp.bfloat16)
            if ph == 0:
                img[2 * n + 1 - pd, 0:rows2, 1] = result
            else:
                img[2 * n + 1 - pd, 1 : rows2 + 1, 0] = result
            return carry

        lax.fori_loop(0, planes2 - 1, plane, 0, unroll=True)

        @pl.when(jnp.logical_not(inside))
        def _():
            outer = 2 * edge + 1 - pd
            if ph == 0:
                img[outer, 0:rows2, 1] = jnp.zeros((rows2,) + img.shape[3:], jnp.bfloat16)
            else:
                img[outer, 1 : rows2 + 1, 0] = jnp.zeros((rows2,) + img.shape[3:], jnp.bfloat16)

    def judge(job):
        def plane(m, carry):
            parts = [
                img[2 * m + kd, kh // 2 : kh // 2 + rows2, kh % 2].reshape(rows2 * cells, 6 * c2)
                for kd in range(4)
                for kh in range(4)
            ]
            total = jnp.dot(
                jnp.concatenate(parts, axis=1), wide3[...], preferred_element_type=jnp.float32
            )
            total = jnp.where(total > 0, total, leak_slope * total)
            count = rows2 * cells
            stage[pl.ds(0, count, stride=2), :] = total[:, :c3]
            stage[pl.ds(1, count, stride=2), :] = total[:, c3:]
            out_ref[job, m] = stage[...].reshape(rows2, 2 * cells, c3).astype(jnp.bfloat16)
            return carry

        lax.fori_loop(0, out_planes, plane, 0)

    half = out_planes // 2

    def swap(r):
        copies = []
        for piece in (0, 1):
            span = pl.ds(piece * half, half)
            copy = pltpu.make_async_remote_copy(
                src_ref=out_ref.at[1, span],
                dst_ref=got.at[r, span],
                send_sem=send_sem.at[piece, r],
                recv_sem=recv_sem.at[piece, r],
                device_id={"trainer": peers[bits[piece][r]]},
                device_id_type=mesh_ids,
            )
            copy.start()
            copies.append(copy)
        return copies

    def settle(r, copies):
        for piece, copy in enumerate(copies):
            copy.wait()
            chosen = jnp.bitwise_and(jnp.right_shift(partner_ref[0], bits[piece][r]), 1) == 1
            for m in range(piece * half, (piece + 1) * half):
                out_ref[1, m] = jnp.where(chosen, got[r, m], out_ref[1, m])

    load(1)
    for index in range(4):
        generate(index)
    judge(1)
    pl.semaphore_wait(barrier, rounds)
    moving = swap(0)
    load(0)
    settled = {(r + 1) * 4 // (rounds - 1) - 1: r for r in range(rounds - 1)}
    for index in range(4):
        generate(index)
        if index in settled:
            settle(settled[index], moving)
            moving = swap(settled[index] + 1)
    judge(0)
    settle(rounds - 1, moving)


def judged_both(partner, parts, second, mate_critic, critic, bits):
    jobs, planes, rows, cells, lanes = parts[0].shape
    count = 2 * (planes - 1)
    rows2 = 2 * rows
    c2 = second.shape[1] // 64
    c1 = second.shape[0]
    c3 = critic.shape[1]
    rounds = len(bits[0])
    flops = 2 * jobs * rows2 * cells * 4 * c2 * ((count + 1) * 4 * 16 * c1 + count * 96 * c2)
    in_vmem = pl.BlockSpec(memory_space=pltpu.VMEM)
    feature_shape = (count, rows2, 2 * cells, c3)
    return pl.pallas_call(
        functools.partial(judged_kernel, bits),
        out_shape=jax.ShapeDtypeStruct((jobs,) + feature_shape, jnp.bfloat16),
        in_specs=[pl.BlockSpec(memory_space=pltpu.SMEM)] + [in_vmem] * 7,
        out_specs=in_vmem,
        scratch_shapes=[
            pltpu.VMEM((count + 2, rows2 + 2, cells, lanes), jnp.bfloat16),
            pltpu.VMEM((4, 4 * lanes, 4 * c2), jnp.bfloat16),
            pltpu.VMEM((2 * count + 2, rows2 + 1, 2, cells, 6 * c2), jnp.bfloat16),
            pltpu.VMEM((96 * c2, 2 * c3), jnp.bfloat16),
            pltpu.VMEM((rows2 * cells * 2, c3), jnp.float32),
            pltpu.VMEM((rounds,) + feature_shape, jnp.bfloat16),
            pltpu.SemaphoreType.DMA((2, rounds)),
            pltpu.SemaphoreType.DMA((2, rounds)),
        ],
        compiler_params=pltpu.CompilerParams(
            vmem_limit_bytes=budget, collective_id=1, has_side_effects=True
        ),
        cost_estimate=pl.CostEstimate(flops=flops, bytes_accessed=2**24, transcendentals=0),
        name="judged",
    )(partner, *parts, second, mate_critic, critic)


def local(latent, gen_first, gen_second, critic, partner):
    rounds = lax.axis_size("trainer").bit_length() - 1
    orders = (
        tuple(range(1, rounds)) + (0,),
        tuple(range(rounds - 1, 0, -1)) + (0,),
    )
    bits = orders[0]
    *parts, second, mate_critic = hidden_parts(
        partner, latent[0], gen_first[0], gen_second[0], critic[0], bits
    )
    second = second.reshape(-1, second.shape[2])
    return judged_both(partner, parts, second, mate_critic, critic[0], orders)[None]


def solution(mesh):
    in_specs = (
        P("trainer", "depth", None, None, None),
        P("trainer", "depth", None),
        P("trainer", "depth", None),
        P("trainer", None, None),
        P(),
    )
    out_specs = P("trainer", None, "depth", None, None, None)
    return jax.shard_map(local, mesh=mesh, in_specs=in_specs, out_specs=out_specs, check_vma=False)
```
